32 devices in a mesh: tm: 4 (over x, core), port: 8 (over z, y).
Axes of the slice: x: 2, y: 2, z: 4, core: 2. Of those that a mesh axis runs over, the one named last changes fastest.
Arguments:
- counters: bfloat16 [4096, 256], P('tm'), may hold values from -6 to 6
- signatures: bfloat16 [256, 8192], P(None, 'port'), may hold values from -0.375 to 0.375
- eigen_vectors_at_pins: bfloat16 [8192, 256], P('port'), may hold values from -0.09375 to 0.09375
- taps: bfloat16 [256, 4096], P('port'), may hold values from -0.5 to 0.5
Outputs:
- voltage_sag: bfloat16 [4096, 8192], P('tm', 'port')
The draws below stay inside these ranges and needn't reach their ends.
All inputs are finite; a program needn't handle non-finite values.
Results may differ from the reference program's by a relative error of at most 0.007.
Values may be sent and summed in bfloat16 or wider, within the bound.
A program may use at most 192 MiB of HBM per device.

```python
import jax
import jax.numpy as jnp
from jax import lax

ACTIVITY_TALLIES = 256
PORTS = 8192
MODES = 256
TAPS = 4096
WINDOW_CYCLES = 4096


def spiked(drawn, key, source, target, blocks, factor):
    def block_of(dim):
        return (jnp.arange(drawn.shape[dim]) // (drawn.shape[dim] // blocks)).reshape((-1,) + (1,) * (drawn.ndim - 1 - dim))

    first = jax.random.permutation(key, blocks)[block_of(target)]
    second = (block_of(target) + blocks // 2) % blocks
    return jnp.where((block_of(source) == first) | (block_of(source) == second), factor * drawn, drawn)


def levels(rng, dims, split, least, high):
    level = 1.0
    for position, blocks in split:
        heights = jax.random.uniform(jax.random.fold_in(jax.random.fold_in(rng, 6), position), (blocks,), jnp.float32, least / len(split), high / len(split))
        level = level * jnp.repeat(jnp.exp(heights), dims[position] // blocks).reshape((-1,) + (1,) * (len(dims) - 1 - position))
    return level


def centred(key, dims, width, bound, shards=(), held_as=jnp.bfloat16):
    result = jax.random.normal(key, dims, jnp.float32) * width
    if len(shards) > 0:
        result = levels(key, dims, shards, -0.22, 0.18) * result
    return jnp.clip(result, min=-bound, max=bound).astype(held_as)


def gaussian_with(rng, shape, width, most, split, heavy, held_as=jnp.bfloat16):
    result = width * jax.random.normal(rng, shape, jnp.float32)
    if split:
        result = result * levels(rng, shape, split, -0.22, 0.18)
    return jnp.clip(spiked(result, jax.random.fold_in(rng, 3), *heavy), -most, most).astype(held_as)


def setup_inputs(seed: int = 0) -> dict:
    streams_of = jax.random.split(jax.random.key(seed), 5)
    return {
        "counters": centred(streams_of[0], (WINDOW_CYCLES, ACTIVITY_TALLIES), 1.0, 6.0, ((0, 4),)),
        "signatures": centred(streams_of[1], (ACTIVITY_TALLIES, PORTS), ACTIVITY_TALLIES ** -0.5, 0.375, ((1, 8),)),
        "eigen_vectors_at_pins": gaussian_with(streams_of[2], (PORTS, MODES), PORTS ** -0.5, 0.09375, ((0, 8),), (0, 1, 8, 2.0)),
        "taps": centred(streams_of[3], (MODES, TAPS), (TAPS * MODES // PORTS) ** -0.5, 0.5, ((0, 8),)),
    }


def reference(counters, signatures, eigen_vectors_at_pins, taps):
    merged = jnp.dot(signatures, eigen_vectors_at_pins, preferred_element_type=jnp.float32)
    projected = jnp.dot(counters.astype(jnp.float32), merged, precision=lax.Precision.HIGHEST)
    modal = lax.optimization_barrier(projected.astype(jnp.bfloat16)).astype(jnp.float32).T
    length = WINDOW_CYCLES + TAPS
    spectrum = jnp.fft.rfft(modal, n=length, axis=1) * jnp.fft.rfft(taps.astype(jnp.float32), n=length, axis=1)
    kernel_taps_per_mode = jnp.fft.irfft(spectrum, n=length, axis=1)[:, :WINDOW_CYCLES].astype(jnp.bfloat16)
    voltage_sag = jnp.dot(kernel_taps_per_mode.T, eigen_vectors_at_pins.T, preferred_element_type=jnp.float32)
    return voltage_sag.astype(jnp.bfloat16)
```

```python
import functools

import jax
import jax.numpy as jnp
import ml_dtypes
import numpy as np
from jax import lax
from jax.experimental import pallas as pl
from jax.experimental.pallas import tpu as pltpu
from jax.sharding import PartitionSpec as P

MESH = pl.DeviceIdType.MESH
F32 = jnp.float32
BF16 = jnp.bfloat16
NT = (((1,), (1,)), ((), ()))
TN = (((0,), (0,)), ((), ()))


def split_parts(x):
    high = x.astype(ml_dtypes.bfloat16)
    low = (x - high.astype(np.float64)).astype(ml_dtypes.bfloat16)
    return high, low


def odd_dft(width):
    theta = np.pi * (2 * np.arange(width) + 1) / (2 * width)
    phase = np.outer(np.arange(width), theta)
    forward = np.concatenate([np.cos(phase), -np.sin(phase)], axis=1)
    phase = np.outer(theta, width + np.arange(width))
    inverse = np.concatenate([np.cos(phase), -np.sin(phase)], axis=0) / width
    return np.concatenate(split_parts(forward), axis=0), np.concatenate(split_parts(inverse), axis=0)


def halves(x):
    high = x.astype(BF16)
    return high, (x - high.astype(F32)).astype(BF16)


def dot(a, b):
    return jnp.dot(a, b, preferred_element_type=F32)


class Plan:
    def __init__(self, tm, port, cycles, ports, tallies, own, span):
        self.tm, self.port, self.cycles, self.ports, self.tallies = tm, port, cycles, ports, tallies
        self.own, self.span = own, span
        self.width = min(256, cycles)
        self.blocks = cycles // self.width
        self.lags = span // self.width
        self.reach = min((span - 2) // cycles + 1, tm - 1)
        self.ways = min(tm, own // 8)
        self.line = port // 2


def response_kernel(
    plan, counters, signatures, eigen, taps, forward, inverse, out,
    cnt, sig, eig, tap, fwd, inv, partial, parts, merged, xs, spectra, taps_spectra, product,
    load_sem, part_send, part_recv, merged_send, merged_recv, modal_send, modal_recv, out_send, out_recv,
):
    T, N, W, C, R, own = plan.tm, plan.port, plan.width, plan.blocks, plan.reach, plan.own
    t, p = lax.axis_index("tm"), lax.axis_index("port")
    loads = [
        pltpu.make_async_copy(src, dst, load_sem.at[i])
        for i, (src, dst) in enumerate(
            [(signatures, sig), (eigen, eig), (forward, fwd), (taps, tap), (counters, cnt), (inverse, inv)]
        )
    ]
    for load in loads:
        load.start()

    barrier = pltpu.get_barrier_semaphore()
    for k in range(1, N):
        pl.semaphore_signal(
            barrier, inc=1, device_id={"tm": t, "port": lax.rem(p + k, N)}, device_id_type=MESH
        )
    greeted = N - 1
    for k in range(1, R + 1):
        @pl.when(t + k < T)
        def _():
            pl.semaphore_signal(barrier, inc=1, device_id={"tm": t + k, "port": p}, device_id_type=MESH)

        @pl.when(t - k >= 0)
        def _():
            pl.semaphore_signal(barrier, inc=1, device_id={"tm": t - k, "port": p}, device_id_type=MESH)

        greeted = greeted + jnp.where(t + k < T, 1, 0) + jnp.where(t - k >= 0, 1, 0)

    loads[0].wait()
    loads[1].wait()
    partial[...] = dot(sig[...], eig[...]).T
    pl.semaphore_wait(barrier, greeted)

    share = lax.rem(t, plan.ways)

    def part_copy(k):
        to = lax.rem(p + k, N)
        return pltpu.make_async_remote_copy(
            src_ref=partial.at[pl.ds(pl.multiple_of(to * own + share * 8, 8), 8)],
            dst_ref=parts.at[k],
            send_sem=part_send.at[k],
            recv_sem=part_recv.at[k],
            device_id={"tm": t, "port": to},
            device_id_type=MESH,
        )

    for k in range(1, N):
        part_copy(k).start()

    loads[2].wait()
    loads[3].wait()

    def transform(x):
        return dot(x, fwd[:W]) + dot(x, fwd[W:])

    quad = 4

    def taps_step(i, carry):
        rows = [
            tap[:, pl.ds(pl.multiple_of((i * quad + j) * W, W), W)] for j in range(quad)
        ]
        result = transform(jnp.concatenate(rows, axis=0))
        taps_spectra[pl.ds(i * quad, quad)] = result.reshape(quad, own, 2 * W)
        return carry

    lax.fori_loop(0, plan.lags // quad, taps_step, 0)
    for d in range(1, R + 1):
        @pl.when(t < d)
        def _():
            xs[d] = jnp.zeros_like(xs[d])

    total = partial[pl.ds(pl.multiple_of(p * own + share * 8, 8), 8)]
    for k in range(1, N):
        part_copy(k).wait_recv()
        total = total + parts[k]
    merged[share] = total

    def merged_copy(k):
        mate = t - share + lax.rem(share + k, plan.ways)
        return pltpu.make_async_remote_copy(
            src_ref=merged.at[share],
            dst_ref=merged.at[share],
            send_sem=merged_send.at[k],
            recv_sem=merged_recv.at[k],
            device_id={"tm": mate, "port": p},
            device_id_type=MESH,
        )

    for k in range(1, plan.ways):
        merged_copy(k).start()
    loads[4].wait()
    for k in range(1, plan.ways):
        came = lax.rem(share + plan.ways - k, plan.ways)
        pltpu.make_async_remote_copy(
            src_ref=merged.at[came], dst_ref=merged.at[came], send_sem=merged_send.at[k],
            recv_sem=merged_recv.at[k], device_id={"tm": t - share + came, "port": p}, device_id_type=MESH,
        ).wait_recv()

    high, low = halves(merged[...].reshape(own, plan.tallies))
    both = lax.dot_general(jnp.concatenate([high, low], axis=0), cnt[...], NT, preferred_element_type=F32)
    xs[0] = (both[:own] + both[own:]).astype(BF16)

    def modal_copy(d):
        return pltpu.make_async_remote_copy(
            src_ref=xs.at[0],
            dst_ref=xs.at[d],
            send_sem=modal_send.at[d],
            recv_sem=modal_recv.at[d],
            device_id={"tm": t + d, "port": p},
            device_id_type=MESH,
        )

    for d in range(1, R + 1):
        @pl.when(t + d < T)
        def _():
            modal_copy(d).start()

    def spectra_of(d):
        rows = jnp.concatenate([xs[d, :, i * W : (i + 1) * W] for i in range(C)], axis=0)
        spectra[(R - d) * C : (R - d + 1) * C] = transform(rows).reshape(C, own, 2 * W)

    spectra_of(0)
    for d in range(1, R + 1):
        @pl.when(t >= d)
        def _():
            modal_copy(d).wait_recv()

        spectra_of(d)

    sign = 1.0 - 2.0 * (lax.broadcasted_iota(jnp.int32, (8, 128), 1) % 2).astype(F32)

    def product_step(g, carry):
        rows = pl.ds(pl.multiple_of(g * 8, 8), 8)
        for q in range(W // 128):
            re, im = slice(q * 128, q * 128 + 128), slice(W + q * 128, W + q * 128 + 128)
            acc_re, acc_im = [None] * C, [None] * C
            before = None
            for j in range(-R * C, C):
                now = (spectra[R * C + j, rows, re], spectra[R * C + j, rows, im])
                z_re, z_im = sign * now[1], -(sign * now[0])
                if before is not None:
                    z_re, z_im = z_re + before[0], z_im + before[1]
                before = now
                for a in range(C):
                    lag = a - j
                    if 0 <= lag < plan.lags:
                        h_re, h_im = taps_spectra[lag, rows, re], taps_spectra[lag, rows, im]
                        add_re, add_im = h_re * z_re - h_im * z_im, h_re * z_im + h_im * z_re
                        acc_re[a] = add_re if acc_re[a] is None else acc_re[a] + add_re
                        acc_im[a] = add_im if acc_im[a] is None else acc_im[a] + add_im
            for a in range(C):
                product[a, rows, re] = acc_re[a]
                product[a, rows, im] = acc_im[a]
        return carry

    lax.fori_loop(0, own // 8, product_step, 0)
    loads[5].wait()
    high, low = halves(product[...].reshape(C * own, 2 * W))
    result = dot(high, inv[: 2 * W]) + dot(low, inv[: 2 * W]) + dot(high, inv[2 * W :])
    out[p] = result.astype(BF16).reshape(C, own, W)

    place, side = p // 2, lax.rem(p, 2)

    def out_copy(piece, c, way, to):
        return pltpu.make_async_remote_copy(
            src_ref=out.at[piece, c],
            dst_ref=out.at[piece, c],
            send_sem=out_send.at[piece, c, way],
            recv_sem=out_recv.at[piece, c],
            device_id={"tm": t, "port": to},
            device_id_type=MESH,
        )

    up, down, partner = 0, 1, 2
    mate = p + 1 - 2 * side

    def send_own(c, carry):
        @pl.when(place + 1 < plan.line)
        def _():
            out_copy(p, c, up, p + 2).start()

        @pl.when(place >= 1)
        def _():
            out_copy(p, c, down, p - 2).start()

        out_copy(p, c, partner, mate).start()
        return carry

    lax.fori_loop(0, C, send_own, 0)
    for k in range(1, plan.line):
        def forward_step(c, carry):
            @pl.when(place >= k)
            def _():
                piece = p - 2 * k
                out_copy(piece, c, up, p).wait_recv()

                @pl.when(place + 1 < plan.line)
                def _():
                    out_copy(piece, c, up, p + 2).start()

                out_copy(piece, c, partner, mate).start()

            @pl.when(place + k < plan.line)
            def _():
                piece = p + 2 * k
                out_copy(piece, c, down, p).wait_recv()

                @pl.when(place >= 1)
                def _():
                    out_copy(piece, c, down, p - 2).start()

                out_copy(piece, c, partner, mate).start()

            return carry

        lax.fori_loop(0, C, forward_step, 0)

    def finish(i, carry):
        c = lax.rem(i, C)
        z = i // C
        out_copy(2 * z + 1 - side, c, partner, mate).wait_recv()
        piece = 2 * z + side
        out_copy(piece, c, partner, mate).wait_send()

        @pl.when((z <= place) & (place + 1 < plan.line))
        def _():
            out_copy(piece, c, up, p).wait_send()

        @pl.when((z >= place) & (place >= 1))
        def _():
            out_copy(piece, c, down, p).wait_send()

        return carry

    lax.fori_loop(0, plan.line * C, finish, 0)
    for k in range(1, N):
        part_copy(k).wait_send()
    for k in range(1, plan.ways):
        merged_copy(k).wait_send()
    for d in range(1, R + 1):
        @pl.when(t + d < T)
        def _():
            modal_copy(d).wait_send()


def response_call(plan, counters, signatures, eigen, taps, forward, inverse):
    T, N, W, C, R, own = plan.tm, plan.port, plan.width, plan.blocks, plan.reach, plan.own
    dma = pltpu.SemaphoreType.DMA
    return pl.pallas_call(
        functools.partial(response_kernel, plan),
        out_shape=jax.ShapeDtypeStruct((N, C, own, W), BF16),
        in_specs=[pl.BlockSpec(memory_space=pl.ANY)] * 6,
        out_specs=pl.BlockSpec(memory_space=pltpu.VMEM),
        scratch_shapes=[
            pltpu.VMEM(counters.shape, BF16),
            pltpu.VMEM(signatures.shape, BF16),
            pltpu.VMEM(eigen.shape, BF16),
            pltpu.VMEM(taps.shape, BF16),
            pltpu.VMEM(forward.shape, BF16),
            pltpu.VMEM(inverse.shape, BF16),
            pltpu.VMEM((N * own, plan.tallies), F32),
            pltpu.VMEM((N, 8, plan.tallies), F32),
            pltpu.VMEM((plan.ways, 8, plan.tallies), F32),
            pltpu.VMEM((R + 1, own, plan.cycles), BF16),
            pltpu.VMEM(((R + 1) * C, own, 2 * W), F32),
            pltpu.VMEM((plan.lags, own, 2 * W), F32),
            pltpu.VMEM((C, own, 2 * W), F32),
            dma((6,)), dma((N,)), dma((N,)), dma((plan.ways,)), dma((plan.ways,)),
            dma((R + 1,)), dma((R + 1,)), dma((N, C, 3)), dma((N, C)),
        ],
        compiler_params=pltpu.CompilerParams(
            collective_id=0, has_side_effects=True, vmem_limit_bytes=32 * 1024 * 1024
        ),
        name="response",
    )(counters, signatures, eigen, taps, forward, inverse)


def output_kernel(plan, response, eigen, out):
    block = response[...].reshape(plan.port * plan.own, plan.width)
    turned = block.T
    out[...] = lax.dot_general(turned, eigen[...], NT, preferred_element_type=F32).astype(BF16)


def output_call(plan, response, eigen):
    return pl.pallas_call(
        functools.partial(output_kernel, plan),
        grid=(plan.blocks,),
        out_shape=jax.ShapeDtypeStruct((plan.cycles, plan.ports), BF16),
        in_specs=[
            pl.BlockSpec((plan.port, None, plan.own, plan.width), lambda a: (0, a, 0, 0)),
            pl.BlockSpec(eigen.shape, lambda a: (0, 0)),
        ],
        out_specs=pl.BlockSpec((plan.width, plan.ports), lambda a: (a, 0)),
        compiler_params=pltpu.CompilerParams(vmem_limit_bytes=24 * 1024 * 1024),
        name="output",
    )(response, eigen)


def solution(mesh):
    def per_device(counters, signatures, eigen, taps):
        plan = Plan(
            mesh.shape["tm"], mesh.shape["port"], counters.shape[0], eigen.shape[0],
            counters.shape[1], taps.shape[0], taps.shape[1],
        )
        forward, inverse = odd_dft(plan.width)
        response = response_call(
            plan, counters, signatures, eigen, taps, jnp.asarray(forward), jnp.asarray(inverse)
        )
        return output_call(plan, response, eigen)

    in_specs = (P("tm", None), P(None, "port"), P("port", None), P("port", None))
    return jax.shard_map(
        per_device, mesh=mesh, in_specs=in_specs, out_specs=P("tm", "port"), check_vma=False
    )
```

```python
import functools

import jax
import jax.numpy as jnp
import ml_dtypes
import numpy as np
from jax import lax
from jax.experimental import pallas as pl
from jax.experimental.pallas import tpu as pltpu
from jax.sharding import PartitionSpec as P

MESH = pl.DeviceIdType.MESH
LARGE_GRANT = 64936 * 1024
F32 = jnp.float32
BF16 = jnp.bfloat16
NT = (((1,), (1,)), ((), ()))
TN = (((0,), (0,)), ((), ()))


def split_parts(x):
    high = x.astype(ml_dtypes.bfloat16)
    low = (x - high.astype(np.float64)).astype(ml_dtypes.bfloat16)
    return high, low


def odd_dft(width):
    theta = np.pi * (2 * np.arange(width) + 1) / (2 * width)
    phase = np.outer(np.arange(width), theta)
    forward = np.concatenate([np.cos(phase), -np.sin(phase)], axis=1)
    phase = np.outer(theta, width + np.arange(width))
    inverse = np.concatenate([np.cos(phase), -np.sin(phase)], axis=0) / width
    return np.concatenate(split_parts(forward), axis=0), np.concatenate(split_parts(inverse), axis=0)


def halves(x):
    high = x.astype(BF16)
    return high, (x - high.astype(F32)).astype(BF16)


def dot(a, b):
    return jnp.dot(a, b, preferred_element_type=F32)


class Plan:
    def __init__(self, tm, port, cycles, ports, tallies, own, span):
        self.tm, self.port, self.cycles, self.ports, self.tallies = tm, port, cycles, ports, tallies
        self.own, self.span = own, span
        self.width = min(256, cycles)
        self.blocks = cycles // self.width
        self.lags = span // self.width
        self.reach = min((span - 2) // cycles + 1, tm - 1)
        self.ways = min(tm, own // 8)
        self.line = port // 2
        self.group = min(16, own)
        self.groups = own // self.group
        self.pieces = 2


def response_kernel(
    plan, counters, signatures, eigen, taps, forward, inverse, out,
    cnt, sig, eig, tap, fwd, inv, partial, parts, merged, xs, spectra, taps_spectra, product,
    load_sem, part_send, part_recv, merged_send, merged_recv, modal_send, modal_recv, out_send, out_recv,
):
    T, N, W, C, R, own = plan.tm, plan.port, plan.width, plan.blocks, plan.reach, plan.own
    G, M = plan.groups, plan.group
    t, p = lax.axis_index("tm"), lax.axis_index("port")
    loads = [
        pltpu.make_async_copy(src, dst, load_sem.at[i])
        for i, (src, dst) in enumerate(
            [(signatures, sig), (eigen, eig), (forward, fwd), (taps, tap), (counters, cnt), (inverse, inv)]
        )
    ]
    for load in loads:
        load.start()

    barrier = pltpu.get_barrier_semaphore()
    for k in range(1, N):
        pl.semaphore_signal(
            barrier, inc=1, device_id={"tm": t, "port": lax.rem(p + k, N)}, device_id_type=MESH
        )
    greeted = N - 1
    for k in range(1, R + 1):
        @pl.when(t + k < T)
        def _():
            pl.semaphore_signal(barrier, inc=1, device_id={"tm": t + k, "port": p}, device_id_type=MESH)

        @pl.when(t - k >= 0)
        def _():
            pl.semaphore_signal(barrier, inc=1, device_id={"tm": t - k, "port": p}, device_id_type=MESH)

        greeted = greeted + jnp.where(t + k < T, 1, 0) + jnp.where(t - k >= 0, 1, 0)

    loads[0].wait()
    loads[1].wait()
    partial[...] = dot(sig[...], eig[...]).T
    pl.semaphore_wait(barrier, greeted)

    share = lax.rem(t, plan.ways)

    def part_copy(k):
        to = lax.rem(p + k, N)
        return pltpu.make_async_remote_copy(
            src_ref=partial.at[pl.ds(pl.multiple_of(to * own + share * 8, 8), 8)],
            dst_ref=parts.at[k],
            send_sem=part_send.at[k],
            recv_sem=part_recv.at[k],
            device_id={"tm": t, "port": to},
            device_id_type=MESH,
        )

    for k in range(1, N):
        part_copy(k).start()

    loads[2].wait()
    loads[3].wait()

    def transform(x):
        return dot(x, fwd[:W]) + dot(x, fwd[W:])

    quad = 4

    def taps_step(i, carry):
        rows = [tap[:, pl.ds(pl.multiple_of((i * quad + j) * W, W), W)] for j in range(quad)]
        result = transform(jnp.concatenate(rows, axis=0))
        taps_spectra[pl.ds(i * quad, quad)] = result.reshape(quad, own, 2 * W)
        return carry

    lax.fori_loop(0, plan.lags // quad, taps_step, 0)
    for d in range(1, R + 1):
        @pl.when(t < d)
        def _():
            xs[d] = jnp.zeros_like(xs[d])

    total = partial[pl.ds(pl.multiple_of(p * own + share * 8, 8), 8)]
    for k in range(1, N):
        part_copy(k).wait_recv()
        total = total + parts[k]
    merged[share] = total

    def merged_copy(k):
        mate = t - share + lax.rem(share + k, plan.ways)
        return pltpu.make_async_remote_copy(
            src_ref=merged.at[share],
            dst_ref=merged.at[share],
            send_sem=merged_send.at[k],
            recv_sem=merged_recv.at[k],
            device_id={"tm": mate, "port": p},
            device_id_type=MESH,
        )

    for k in range(1, plan.ways):
        merged_copy(k).start()
    loads[4].wait()
    for k in range(1, plan.ways):
        came = lax.rem(share + plan.ways - k, plan.ways)
        pltpu.make_async_remote_copy(
            src_ref=merged.at[came], dst_ref=merged.at[came], send_sem=merged_send.at[k],
            recv_sem=merged_recv.at[k], device_id={"tm": t - share + came, "port": p}, device_id_type=MESH,
        ).wait_recv()

    high, low = halves(merged[...].reshape(own, plan.tallies))
    both = lax.dot_general(jnp.concatenate([high, low], axis=0), cnt[...], NT, preferred_element_type=F32)
    modal = (both[:own] + both[own:]).astype(BF16)
    xs[0] = modal.reshape(G, M, plan.cycles)

    def modal_copy(d, h):
        return pltpu.make_async_remote_copy(
            src_ref=xs.at[0, h],
            dst_ref=xs.at[d, h],
            send_sem=modal_send.at[d, h],
            recv_sem=modal_recv.at[d, h],
            device_id={"tm": t + d, "port": p},
            device_id_type=MESH,
        )

    for h in range(G):
        for d in range(1, R + 1):
            @pl.when(t + d < T)
            def _():
                modal_copy(d, h).start()

    sign = 1.0 - 2.0 * (lax.broadcasted_iota(jnp.int32, (8, 128), 1) % 2).astype(F32)

    def product_step(h, g):
        rows = pl.ds(pl.multiple_of(g * 8, 8), 8)
        taps_rows = pl.ds(pl.multiple_of(h * M + g * 8, 8), 8)
        for q in range(W // 128):
            re, im = slice(q * 128, q * 128 + 128), slice(W + q * 128, W + q * 128 + 128)
            acc_re, acc_im = [None] * C, [None] * C
            before = None
            for j in range(-R * C, C):
                now = (spectra[R * C + j, rows, re], spectra[R * C + j, rows, im])
                z_re, z_im = sign * now[1], -(sign * now[0])
                if before is not None:
                    z_re, z_im = z_re + before[0], z_im + before[1]
                before = now
                for a in range(C):
                    lag = a - j
                    if 0 <= lag < plan.lags:
                        h_re, h_im = taps_spectra[lag, taps_rows, re], taps_spectra[lag, taps_rows, im]
                        add_re, add_im = h_re * z_re - h_im * z_im, h_re * z_im + h_im * z_re
                        acc_re[a] = add_re if acc_re[a] is None else acc_re[a] + add_re
                        acc_im[a] = add_im if acc_im[a] is None else acc_im[a] + add_im
            for a in range(C):
                product[a, rows, re] = acc_re[a]
                product[a, rows, im] = acc_im[a]

    place, side = p // 2, lax.rem(p, 2)
    S = plan.pieces
    wide = plan.cycles // S
    up, down, partner = 0, 1, 2
    mate = p + 1 - 2 * side

    def out_copy(piece, i, way, to):
        h = i // S
        c = lax.rem(i, S)
        part = out.at[piece, h, :, pl.ds(pl.multiple_of(c * wide, wide), wide)]
        return pltpu.make_async_remote_copy(
            src_ref=part,
            dst_ref=part,
            send_sem=out_send.at[piece, i, way],
            recv_sem=out_recv.at[piece, i],
            device_id={"tm": t, "port": to},
            device_id_type=MESH,
        )

    loads[5].wait()

    def group_step(h, carry):
        for d in range(1, R + 1):
            @pl.when(t >= d)
            def _():
                modal_copy(d, h).wait_recv()

        rows = [
            xs[d, h, :, i * W : (i + 1) * W] for d in range(R, -1, -1) for i in range(C)
        ]
        spectra[...] = transform(jnp.concatenate(rows, axis=0)).reshape((R + 1) * C, M, 2 * W)

        def step(g, inner):
            product_step(h, g)
            return inner

        lax.fori_loop(0, M // 8, step, 0)
        high, low = halves(product[...].reshape(C * M, 2 * W))
        result = dot(high, inv[: 2 * W]) + dot(low, inv[: 2 * W]) + dot(high, inv[2 * W :])
        result = result.astype(BF16)
        for a in range(C):
            out[p, h, :, a * W : (a + 1) * W] = result[a * M : (a + 1) * M]

        for c in range(S):
            i = h * S + c

            @pl.when(place + 1 < plan.line)
            def _():
                out_copy(p, i, up, p + 2).start()

            @pl.when(place >= 1)
            def _():
                out_copy(p, i, down, p - 2).start()

            out_copy(p, i, partner, mate).start()

        return carry

    lax.fori_loop(0, G, group_step, 0)

    for k in range(1, plan.line):
        def forward_step(i, carry):
            @pl.when(place >= k)
            def _():
                piece = p - 2 * k
                out_copy(piece, i, up, p).wait_recv()

                @pl.when(place + 1 < plan.line)
                def _():
                    out_copy(piece, i, up, p + 2).start()

                out_copy(piece, i, partner, mate).start()

            @pl.when(place + k < plan.line)
            def _():
                piece = p + 2 * k
                out_copy(piece, i, down, p).wait_recv()

                @pl.when(place >= 1)
                def _():
                    out_copy(piece, i, down, p - 2).start()

                out_copy(piece, i, partner, mate).start()

            return carry

        lax.fori_loop(0, G * S, forward_step, 0)

    def finish(i, carry):
        c = lax.rem(i, G * S)
        z = i // (G * S)
        out_copy(2 * z + 1 - side, c, partner, mate).wait_recv()
        piece = 2 * z + side
        out_copy(piece, c, partner, mate).wait_send()

        @pl.when((z <= place) & (place + 1 < plan.line))
        def _():
            out_copy(piece, c, up, p).wait_send()

        @pl.when((z >= place) & (place >= 1))
        def _():
            out_copy(piece, c, down, p).wait_send()

        return carry

    lax.fori_loop(0, plan.line * G * S, finish, 0)
    for k in range(1, N):
        part_copy(k).wait_send()
    for k in range(1, plan.ways):
        merged_copy(k).wait_send()
    for d in range(1, R + 1):
        @pl.when(t + d < T)
        def _():
            for h in range(G):
                modal_copy(d, h).wait_send()


def response_call(plan, counters, signatures, eigen, taps, forward, inverse):
    T, N, W, C, R, own = plan.tm, plan.port, plan.width, plan.blocks, plan.reach, plan.own
    G, M, S = plan.groups, plan.group, plan.pieces
    dma = pltpu.SemaphoreType.DMA
    return pl.pallas_call(
        functools.partial(response_kernel, plan),
        out_shape=jax.ShapeDtypeStruct((N, G, M, plan.cycles), BF16),
        in_specs=[pl.BlockSpec(memory_space=pl.ANY)] * 6,
        out_specs=pl.BlockSpec(memory_space=pltpu.VMEM),
        scratch_shapes=[
            pltpu.VMEM(counters.shape, BF16),
            pltpu.VMEM(signatures.shape, BF16),
            pltpu.VMEM(eigen.shape, BF16),
            pltpu.VMEM(taps.shape, BF16),
            pltpu.VMEM(forward.shape, BF16),
            pltpu.VMEM(inverse.shape, BF16),
            pltpu.VMEM((N * own, plan.tallies), F32),
            pltpu.VMEM((N, 8, plan.tallies), F32),
            pltpu.VMEM((plan.ways, 8, plan.tallies), F32),
            pltpu.VMEM((R + 1, G, M, plan.cycles), BF16),
            pltpu.VMEM(((R + 1) * C, M, 2 * W), F32),
            pltpu.VMEM((plan.lags, own, 2 * W), F32),
            pltpu.VMEM((C, M, 2 * W), F32),
            dma((6,)), dma((N,)), dma((N,)), dma((plan.ways,)), dma((plan.ways,)),
            dma((R + 1, G)), dma((R + 1, G)), dma((N, G * S, 3)), dma((N, G * S)),
        ],
        compiler_params=pltpu.CompilerParams(
            collective_id=0, has_side_effects=True, vmem_limit_bytes=LARGE_GRANT
        ),
        name="response",
    )(counters, signatures, eigen, taps, forward, inverse)


def output_kernel(plan, response, eigen, out):
    block = response[...].reshape(plan.port * plan.own, plan.width)
    turned = block.T
    out[...] = lax.dot_general(turned, eigen[...], NT, preferred_element_type=F32).astype(BF16)


def output_call(plan, response, eigen):
    return pl.pallas_call(
        functools.partial(output_kernel, plan),
        grid=(plan.blocks,),
        out_shape=jax.ShapeDtypeStruct((plan.cycles, plan.ports), BF16),
        in_specs=[
            pl.BlockSpec((plan.port, plan.groups, plan.group, plan.width), lambda a: (0, 0, 0, a)),
            pl.BlockSpec(eigen.shape, lambda a: (0, 0)),
        ],
        out_specs=pl.BlockSpec((plan.width, plan.ports), lambda a: (a, 0)),
        compiler_params=pltpu.CompilerParams(vmem_limit_bytes=LARGE_GRANT),
        name="output",
    )(response, eigen)


def solution(mesh):
    def per_device(counters, signatures, eigen, taps):
        plan = Plan(
            mesh.shape["tm"], mesh.shape["port"], counters.shape[0], eigen.shape[0],
            counters.shape[1], taps.shape[0], taps.shape[1],
        )
        forward, inverse = odd_dft(plan.width)
        response = response_call(
            plan, counters, signatures, eigen, taps, jnp.asarray(forward), jnp.asarray(inverse)
        )
        return output_call(plan, response, eigen)

    in_specs = (P("tm", None), P(None, "port"), P("port", None), P("port", None))
    return jax.shard_map(
        per_device, mesh=mesh, in_specs=in_specs, out_specs=P("tm", "port"), check_vma=False
    )
```

```python
import functools

import jax
import jax.numpy as jnp
import ml_dtypes
import numpy as np
from jax import lax
from jax.experimental import pallas as pl
from jax.experimental.pallas import tpu as pltpu
from jax.sharding import PartitionSpec as P

MESH = pl.DeviceIdType.MESH
LARGE_GRANT = 60 * 1024 * 1024
F32 = jnp.float32
BF16 = jnp.bfloat16
NT = (((1,), (1,)), ((), ()))
TN = (((0,), (0,)), ((), ()))


def split_parts(x):
    high = x.astype(ml_dtypes.bfloat16)
    low = (x - high.astype(np.float64)).astype(ml_dtypes.bfloat16)
    return high, low


def odd_dft(width):
    theta = np.pi * (2 * np.arange(width) + 1) / (2 * width)
    phase = np.outer(np.arange(width), theta)
    forward = np.concatenate([np.cos(phase), -np.sin(phase)], axis=1)
    phase = np.outer(theta, width + np.arange(width))
    inverse = np.concatenate([np.cos(phase), -np.sin(phase)], axis=0) / width
    return np.concatenate(split_parts(forward), axis=0), np.concatenate(split_parts(inverse), axis=0)


def halves(x):
    high = x.astype(BF16)
    return high, (x - high.astype(F32)).astype(BF16)


def dot(a, b):
    return jnp.dot(a, b, preferred_element_type=F32)


class Plan:
    def __init__(self, tm, port, cycles, ports, tallies, own, span):
        self.tm, self.port, self.cycles, self.ports, self.tallies = tm, port, cycles, ports, tallies
        self.own, self.span = own, span
        self.width = min(256, cycles)
        self.blocks = cycles // self.width
        self.lags = span // self.width
        self.reach = min((span - 2) // cycles + 1, tm - 1)
        self.ways = min(tm, own // 8)
        self.rows = own // self.ways
        self.line = port // 2
        self.group = min(16, own)
        self.groups = own // self.group
        self.pieces = 2


def response_kernel(
    plan, counters, signatures, eigen, taps, forward, inverse, out,
    cnt, sig, eig, tap, fwd, inv, partial, parts, merged, xs, spectra, taps_spectra, product,
    load_sem, part_send, part_recv, merged_send, merged_recv, modal_send, modal_recv, out_send, out_recv,
):
    T, N, W, C, R, own = plan.tm, plan.port, plan.width, plan.blocks, plan.reach, plan.own
    G, M = plan.groups, plan.group
    t, p = lax.axis_index("tm"), lax.axis_index("port")
    loads = [
        pltpu.make_async_copy(src, dst, load_sem.at[i])
        for i, (src, dst) in enumerate(
            [(signatures, sig), (eigen, eig), (forward, fwd), (taps, tap), (counters, cnt), (inverse, inv)]
        )
    ]
    for load in loads:
        load.start()

    barrier = pltpu.get_barrier_semaphore()
    for k in range(1, N):
        pl.semaphore_signal(
            barrier, inc=1, device_id={"tm": t, "port": lax.rem(p + k, N)}, device_id_type=MESH
        )
    greeted = N - 1
    for k in range(1, R + 1):
        @pl.when(t + k < T)
        def _():
            pl.semaphore_signal(barrier, inc=1, device_id={"tm": t + k, "port": p}, device_id_type=MESH)

        @pl.when(t - k >= 0)
        def _():
            pl.semaphore_signal(barrier, inc=1, device_id={"tm": t - k, "port": p}, device_id_type=MESH)

        greeted = greeted + jnp.where(t + k < T, 1, 0) + jnp.where(t - k >= 0, 1, 0)

    loads[0].wait()
    loads[1].wait()
    partial[...] = dot(sig[...], eig[...]).T
    pl.semaphore_wait(barrier, greeted)

    share = lax.rem(t, plan.ways)

    def part_copy(k):
        to = lax.rem(p + k, N)
        return pltpu.make_async_remote_copy(
            src_ref=partial.at[pl.ds(pl.multiple_of(to * own + share * plan.rows, 8), plan.rows)],
            dst_ref=parts.at[k],
            send_sem=part_send.at[k],
            recv_sem=part_recv.at[k],
            device_id={"tm": t, "port": to},
            device_id_type=MESH,
        )

    for k in range(1, N):
        part_copy(k).start()

    loads[2].wait()
    loads[3].wait()

    def transform(x):
        return dot(x, fwd[:W]) + dot(x, fwd[W:])

    quad = 4

    def taps_step(i, carry):
        rows = [tap[:, pl.ds(pl.multiple_of((i * quad + j) * W, W), W)] for j in range(quad)]
        result = transform(jnp.concatenate(rows, axis=0))
        taps_spectra[pl.ds(i * quad, quad)] = result.reshape(quad, own, 2 * W)
        return carry

    lax.fori_loop(0, plan.lags // quad, taps_step, 0)
    for d in range(1, R + 1):
        @pl.when(t < d)
        def _():
            xs[d] = jnp.zeros_like(xs[d])

    total = partial[pl.ds(pl.multiple_of(p * own + share * plan.rows, 8), plan.rows)]
    for k in range(1, N):
        part_copy(k).wait_recv()
        total = total + parts[k]
    merged[share] = total

    def merged_copy(k):
        mate = t - share + lax.rem(share + k, plan.ways)
        return pltpu.make_async_remote_copy(
            src_ref=merged.at[share],
            dst_ref=merged.at[share],
            send_sem=merged_send.at[k],
            recv_sem=merged_recv.at[k],
            device_id={"tm": mate, "port": p},
            device_id_type=MESH,
        )

    for k in range(1, plan.ways):
        merged_copy(k).start()
    loads[4].wait()
    for k in range(1, plan.ways):
        came = lax.rem(share + plan.ways - k, plan.ways)
        pltpu.make_async_remote_copy(
            src_ref=merged.at[came], dst_ref=merged.at[came], send_sem=merged_send.at[k],
            recv_sem=merged_recv.at[k], device_id={"tm": t - share + came, "port": p}, device_id_type=MESH,
        ).wait_recv()

    high, low = halves(merged[...].reshape(own, plan.tallies))
    both = lax.dot_general(jnp.concatenate([high, low], axis=0), cnt[...], NT, preferred_element_type=F32)
    modal = (both[:own] + both[own:]).astype(BF16)
    xs[0] = modal.reshape(G, M, plan.cycles)

    def modal_copy(d, h):
        return pltpu.make_async_remote_copy(
            src_ref=xs.at[0, h],
            dst_ref=xs.at[d, h],
            send_sem=modal_send.at[d, h],
            recv_sem=modal_recv.at[d, h],
            device_id={"tm": t + d, "port": p},
            device_id_type=MESH,
        )

    for h in range(G):
        for d in range(1, R + 1):
            @pl.when(t + d < T)
            def _():
                modal_copy(d, h).start()

    sign = 1.0 - 2.0 * (lax.broadcasted_iota(jnp.int32, (8, 128), 1) % 2).astype(F32)

    def product_step(h, g):
        rows = pl.ds(pl.multiple_of(g * 8, 8), 8)
        taps_rows = pl.ds(pl.multiple_of(h * M + g * 8, 8), 8)
        for q in range(W // 128):
            re, im = slice(q * 128, q * 128 + 128), slice(W + q * 128, W + q * 128 + 128)
            acc_re, acc_im = [None] * C, [None] * C
            before = None
            for j in range(-R * C, C):
                now = (spectra[R * C + j, rows, re], spectra[R * C + j, rows, im])
                z_re, z_im = sign * now[1], -(sign * now[0])
                if before is not None:
                    z_re, z_im = z_re + before[0], z_im + before[1]
                before = now
                for a in range(C):
                    lag = a - j
                    if 0 <= lag < plan.lags:
                        h_re, h_im = taps_spectra[lag, taps_rows, re], taps_spectra[lag, taps_rows, im]
                        add_re, add_im = h_re * z_re - h_im * z_im, h_re * z_im + h_im * z_re
                        acc_re[a] = add_re if acc_re[a] is None else acc_re[a] + add_re
                        acc_im[a] = add_im if acc_im[a] is None else acc_im[a] + add_im
            for a in range(C):
                product[a, rows, re] = acc_re[a]
                product[a, rows, im] = acc_im[a]

    place, side = p // 2, lax.rem(p, 2)
    S = plan.pieces
    wide = plan.cycles // S
    partner = 0
    mate = p + 1 - 2 * side

    def out_copy(piece, i, way, to):
        h = i // S
        c = lax.rem(i, S)
        part = out.at[piece, h, :, pl.ds(pl.multiple_of(c * wide, wide), wide)]
        return pltpu.make_async_remote_copy(
            src_ref=part,
            dst_ref=part,
            send_sem=out_send.at[piece, i, way],
            recv_sem=out_recv.at[piece, i],
            device_id={"tm": t, "port": to},
            device_id_type=MESH,
        )

    loads[5].wait()

    def group_step(h, carry):
        for d in range(1, R + 1):
            @pl.when(t >= d)
            def _():
                modal_copy(d, h).wait_recv()

        rows = [
            xs[d, h, :, i * W : (i + 1) * W] for d in range(R, -1, -1) for i in range(C)
        ]
        spectra[...] = transform(jnp.concatenate(rows, axis=0)).reshape((R + 1) * C, M, 2 * W)

        def step(g, inner):
            product_step(h, g)
            return inner

        lax.fori_loop(0, M // 8, step, 0)
        high, low = halves(product[...].reshape(C * M, 2 * W))
        result = dot(high, inv[: 2 * W]) + dot(low, inv[: 2 * W]) + dot(high, inv[2 * W :])
        result = result.astype(BF16)
        for a in range(C):
            out[p, h, :, a * W : (a + 1) * W] = result[a * M : (a + 1) * M]

        for c in range(S):
            i = h * S + c

            for k in range(1, plan.line):
                @pl.when(place + k < plan.line)
                def _():
                    out_copy(p, i, k, p + 2 * k).start()

                @pl.when(place >= k)
                def _():
                    out_copy(p, i, plan.line + k, p - 2 * k).start()

            out_copy(p, i, partner, mate).start()

        return carry

    lax.fori_loop(0, G, group_step, 0)

    for k in range(1, plan.line):
        def forward_step(i, carry):
            for there, piece in ((place >= k, p - 2 * k), (place + k < plan.line, p + 2 * k)):
                @pl.when(there)
                def _():
                    out_copy(piece, i, partner, mate).wait_recv()
                    out_copy(piece, i, partner, mate).start()

            return carry

        lax.fori_loop(0, G * S, forward_step, 0)

    def finish(i, carry):
        c = lax.rem(i, G * S)
        z = i // (G * S)
        out_copy(2 * z + 1 - side, c, partner, mate).wait_recv()
        piece = 2 * z + side
        out_copy(piece, c, partner, mate).wait_send()

        return carry

    lax.fori_loop(0, plan.line * G * S, finish, 0)
    for k in range(1, plan.line):
        def sent(i, carry):
            @pl.when(place + k < plan.line)
            def _():
                out_copy(p, i, k, p + 2 * k).wait_send()

            @pl.when(place >= k)
            def _():
                out_copy(p, i, plan.line + k, p - 2 * k).wait_send()

            return carry

        lax.fori_loop(0, G * S, sent, 0)
    for k in range(1, N):
        part_copy(k).wait_send()
    for k in range(1, plan.ways):
        merged_copy(k).wait_send()
    for d in range(1, R + 1):
        @pl.when(t + d < T)
        def _():
            for h in range(G):
                modal_copy(d, h).wait_send()


def response_call(plan, counters, signatures, eigen, taps, forward, inverse):
    T, N, W, C, R, own = plan.tm, plan.port, plan.width, plan.blocks, plan.reach, plan.own
    G, M, S = plan.groups, plan.group, plan.pieces
    dma = pltpu.SemaphoreType.DMA
    return pl.pallas_call(
        functools.partial(response_kernel, plan),
        out_shape=jax.ShapeDtypeStruct((N, G, M, plan.cycles), BF16),
        in_specs=[pl.BlockSpec(memory_space=pl.ANY)] * 6,
        out_specs=pl.BlockSpec(memory_space=pltpu.VMEM),
        scratch_shapes=[
            pltpu.VMEM(counters.shape, BF16),
            pltpu.VMEM(signatures.shape, BF16),
            pltpu.VMEM(eigen.shape, BF16),
            pltpu.VMEM(taps.shape, BF16),
            pltpu.VMEM(forward.shape, BF16),
            pltpu.VMEM(inverse.shape, BF16),
            pltpu.VMEM((N * own, plan.tallies), F32),
            pltpu.VMEM((N, plan.rows, plan.tallies), F32),
            pltpu.VMEM((plan.ways, plan.rows, plan.tallies), F32),
            pltpu.VMEM((R + 1, G, M, plan.cycles), BF16),
            pltpu.VMEM(((R + 1) * C, M, 2 * W), F32),
            pltpu.VMEM((plan.lags, own, 2 * W), F32),
            pltpu.VMEM((C, M, 2 * W), F32),
            dma((6,)), dma((N,)), dma((N,)), dma((plan.ways,)), dma((plan.ways,)),
            dma((R + 1, G)), dma((R + 1, G)), dma((N, G * S, 2 * plan.line)), dma((N, G * S)),
        ],
        compiler_params=pltpu.CompilerParams(
            collective_id=0, has_side_effects=True, vmem_limit_bytes=LARGE_GRANT
        ),
        name="response",
    )(counters, signatures, eigen, taps, forward, inverse)


def output_kernel(plan, response, eigen, out):
    block = response[...].reshape(plan.port * plan.own, plan.width)
    turned = block.T
    out[...] = lax.dot_general(turned, eigen[...], NT, preferred_element_type=F32).astype(BF16)


def output_call(plan, response, eigen):
    return pl.pallas_call(
        functools.partial(output_kernel, plan),
        grid=(plan.blocks,),
        out_shape=jax.ShapeDtypeStruct((plan.cycles, plan.ports), BF16),
        in_specs=[
            pl.BlockSpec((plan.port, plan.groups, plan.group, plan.width), lambda a: (0, 0, 0, a)),
            pl.BlockSpec(eigen.shape, lambda a: (0, 0)),
        ],
        out_specs=pl.BlockSpec((plan.width, plan.ports), lambda a: (a, 0)),
        compiler_params=pltpu.CompilerParams(vmem_limit_bytes=24 * 1024 * 1024),
        name="output",
    )(response, eigen)


def solution(mesh):
    def per_device(counters, signatures, eigen, taps):
        plan = Plan(
            mesh.shape["tm"], mesh.shape["port"], counters.shape[0], eigen.shape[0],
            counters.shape[1], taps.shape[0], taps.shape[1],
        )
        forward, inverse = odd_dft(plan.width)
        response = response_call(
            plan, counters, signatures, eigen, taps, jnp.asarray(forward), jnp.asarray(inverse)
        )
        return output_call(plan, response, eigen)

    in_specs = (P("tm", None), P(None, "port"), P("port", None), P("port", None))
    return jax.shard_map(
        per_device, mesh=mesh, in_specs=in_specs, out_specs=P("tm", "port"), check_vma=False
    )
```

```python
import functools

import jax
import jax.numpy as jnp
import ml_dtypes
import numpy as np
from jax import lax
from jax.experimental import pallas as pl
from jax.experimental.pallas import tpu as pltpu
from jax.sharding import PartitionSpec as P

MESH = pl.DeviceIdType.MESH
LARGE_GRANT = 60 * 1024 * 1024
F32 = jnp.float32
BF16 = jnp.bfloat16
NT = (((1,), (1,)), ((), ()))
TN = (((0,), (0,)), ((), ()))


def split_parts(x):
    high = x.astype(ml_dtypes.bfloat16)
    low = (x - high.astype(np.float64)).astype(ml_dtypes.bfloat16)
    return high, low


def odd_dft(width):
    theta = np.pi * (2 * np.arange(width) + 1) / (2 * width)
    phase = np.outer(np.arange(width), theta)
    forward = np.concatenate([np.cos(phase), -np.sin(phase)], axis=1)
    phase = np.outer(theta, width + np.arange(width))
    inverse = np.concatenate([np.cos(phase), -np.sin(phase)], axis=0) / width
    return np.concatenate(split_parts(forward), axis=0), np.concatenate(split_parts(inverse), axis=0)


def halves(x):
    high = x.astype(BF16)
    return high, (x - high.astype(F32)).astype(BF16)


def dot(a, b):
    return jnp.dot(a, b, preferred_element_type=F32)


class Plan:
    def __init__(self, tm, port, cycles, ports, tallies, own, span):
        self.tm, self.port, self.cycles, self.ports, self.tallies = tm, port, cycles, ports, tallies
        self.own, self.span = own, span
        self.width = min(256, cycles)
        self.blocks = cycles // self.width
        self.lags = span // self.width
        self.reach = min((span - 2) // cycles + 1, tm - 1)
        self.ways = min(tm, own // 8)
        self.rows = own // self.ways
        self.line = port // 2
        self.group = min(16, own)
        self.groups = own // self.group
        self.pieces = 2


def sag_kernel(
    plan, counters, signatures, eigen, taps, forward, inverse, sag,
    cnt, sig, eig, tap, fwd, inv, partial, parts, merged, xs, spectra, taps_spectra, product, out, turned, total, rounded,
    load_sem, part_send, part_recv, merged_send, merged_recv, modal_send, modal_recv, out_send, out_recv, sag_sem,
):
    T, N, W, C, R, own = plan.tm, plan.port, plan.width, plan.blocks, plan.reach, plan.own
    G, M = plan.groups, plan.group
    t, p = lax.axis_index("tm"), lax.axis_index("port")
    loads = [
        pltpu.make_async_copy(src, dst, load_sem.at[i])
        for i, (src, dst) in enumerate(
            [(signatures, sig), (eigen, eig), (forward, fwd), (taps, tap), (counters, cnt), (inverse, inv)]
        )
    ]
    for load in loads:
        load.start()

    barrier = pltpu.get_barrier_semaphore()
    for k in range(1, N):
        pl.semaphore_signal(
            barrier, inc=1, device_id={"tm": t, "port": lax.rem(p + k, N)}, device_id_type=MESH
        )
    greeted = N - 1
    for k in range(1, R + 1):
        @pl.when(t + k < T)
        def _():
            pl.semaphore_signal(barrier, inc=1, device_id={"tm": t + k, "port": p}, device_id_type=MESH)

        @pl.when(t - k >= 0)
        def _():
            pl.semaphore_signal(barrier, inc=1, device_id={"tm": t - k, "port": p}, device_id_type=MESH)

        greeted = greeted + jnp.where(t + k < T, 1, 0) + jnp.where(t - k >= 0, 1, 0)

    loads[0].wait()
    loads[1].wait()
    partial[...] = dot(sig[...], eig[...]).T
    pl.semaphore_wait(barrier, greeted)

    share = lax.rem(t, plan.ways)

    def part_copy(k):
        to = lax.rem(p + k, N)
        return pltpu.make_async_remote_copy(
            src_ref=partial.at[pl.ds(pl.multiple_of(to * own + share * plan.rows, 8), plan.rows)],
            dst_ref=parts.at[k],
            send_sem=part_send.at[k],
            recv_sem=part_recv.at[k],
            device_id={"tm": t, "port": to},
            device_id_type=MESH,
        )

    for k in range(1, N):
        part_copy(k).start()

    loads[2].wait()
    loads[3].wait()

    def transform(x):
        return dot(x, fwd[:W]) + dot(x, fwd[W:])

    quad = 4

    def taps_step(i, carry):
        rows = [tap[:, pl.ds(pl.multiple_of((i * quad + j) * W, W), W)] for j in range(quad)]
        result = transform(jnp.concatenate(rows, axis=0))
        taps_spectra[pl.ds(i * quad, quad)] = result.reshape(quad, own, 2 * W)
        return carry

    lax.fori_loop(0, plan.lags // quad, taps_step, 0)
    tile = min(256, plan.ports)
    for i in range(plan.ports // tile):
        block = eig[i * tile : (i + 1) * tile].T
        for piece in range(N):
            z, b = divmod(piece, 2)
            turned[b, z * own : (z + 1) * own, i * tile : (i + 1) * tile] = block[piece * own : (piece + 1) * own]
    for d in range(1, R + 1):
        @pl.when(t < d)
        def _():
            xs[d] = jnp.zeros_like(xs[d])

    octet = partial[pl.ds(pl.multiple_of(p * own + share * plan.rows, 8), plan.rows)]
    for k in range(1, N):
        part_copy(k).wait_recv()
        octet = octet + parts[k]
    merged[share] = octet

    def merged_copy(k):
        mate = t - share + lax.rem(share + k, plan.ways)
        return pltpu.make_async_remote_copy(
            src_ref=merged.at[share],
            dst_ref=merged.at[share],
            send_sem=merged_send.at[k],
            recv_sem=merged_recv.at[k],
            device_id={"tm": mate, "port": p},
            device_id_type=MESH,
        )

    for k in range(1, plan.ways):
        merged_copy(k).start()
    loads[4].wait()
    for k in range(1, plan.ways):
        came = lax.rem(share + plan.ways - k, plan.ways)
        pltpu.make_async_remote_copy(
            src_ref=merged.at[came], dst_ref=merged.at[came], send_sem=merged_send.at[k],
            recv_sem=merged_recv.at[k], device_id={"tm": t - share + came, "port": p}, device_id_type=MESH,
        ).wait_recv()

    high, low = halves(merged[...].reshape(own, plan.tallies))
    both = lax.dot_general(jnp.concatenate([high, low], axis=0), cnt[...], NT, preferred_element_type=F32)
    modal = (both[:own] + both[own:]).astype(BF16)
    xs[0] = modal.reshape(G, M, plan.cycles)

    def modal_copy(d, h):
        return pltpu.make_async_remote_copy(
            src_ref=xs.at[0, h],
            dst_ref=xs.at[d, h],
            send_sem=modal_send.at[d, h],
            recv_sem=modal_recv.at[d, h],
            device_id={"tm": t + d, "port": p},
            device_id_type=MESH,
        )

    for h in range(G):
        for d in range(1, R + 1):
            @pl.when(t + d < T)
            def _():
                modal_copy(d, h).start()

    sign = 1.0 - 2.0 * (lax.broadcasted_iota(jnp.int32, (8, 128), 1) % 2).astype(F32)

    def product_step(h, g):
        rows = pl.ds(pl.multiple_of(g * 8, 8), 8)
        taps_rows = pl.ds(pl.multiple_of(h * M + g * 8, 8), 8)
        for q in range(W // 128):
            re, im = slice(q * 128, q * 128 + 128), slice(W + q * 128, W + q * 128 + 128)
            acc_re, acc_im = [None] * C, [None] * C
            before = None
            for j in range(-R * C, C):
                now = (spectra[R * C + j, rows, re], spectra[R * C + j, rows, im])
                z_re, z_im = sign * now[1], -(sign * now[0])
                if before is not None:
                    z_re, z_im = z_re + before[0], z_im + before[1]
                before = now
                for a in range(C):
                    lag = a - j
                    if 0 <= lag < plan.lags:
                        h_re, h_im = taps_spectra[lag, taps_rows, re], taps_spectra[lag, taps_rows, im]
                        add_re, add_im = h_re * z_re - h_im * z_im, h_re * z_im + h_im * z_re
                        acc_re[a] = add_re if acc_re[a] is None else acc_re[a] + add_re
                        acc_im[a] = add_im if acc_im[a] is None else acc_im[a] + add_im
            for a in range(C):
                product[a, rows, re] = acc_re[a]
                product[a, rows, im] = acc_im[a]

    place, side = p // 2, lax.rem(p, 2)
    S = plan.pieces
    wide = plan.cycles // S
    up, down, partner, across = 0, 1, 2, 3
    mate = p + 1 - 2 * side
    pair = place + 1 - 2 * lax.rem(place, 2)
    paired = 2 * pair + side

    def out_copy(piece, i, way, to):
        h = i // S
        c = lax.rem(i, S)
        part = out.at[lax.rem(piece, 2), piece // 2, h, :, pl.ds(pl.multiple_of(c * wide, wide), wide)]
        return pltpu.make_async_remote_copy(
            src_ref=part,
            dst_ref=part,
            send_sem=out_send.at[piece, i, way],
            recv_sem=out_recv.at[piece, i],
            device_id={"tm": t, "port": to},
            device_id_type=MESH,
        )

    loads[5].wait()

    def group_step(h, carry):
        for d in range(1, R + 1):
            @pl.when(t >= d)
            def _():
                modal_copy(d, h).wait_recv()

        rows = [
            xs[d, h, :, i * W : (i + 1) * W] for d in range(R, -1, -1) for i in range(C)
        ]
        spectra[...] = transform(jnp.concatenate(rows, axis=0)).reshape((R + 1) * C, M, 2 * W)

        def step(g, inner):
            product_step(h, g)
            return inner

        lax.fori_loop(0, M // 8, step, 0)
        high, low = halves(product[...].reshape(C * M, 2 * W))
        result = dot(high, inv[: 2 * W]) + dot(low, inv[: 2 * W]) + dot(high, inv[2 * W :])
        result = result.astype(BF16)
        for a in range(C):
            out[side, place, h, :, a * W : (a + 1) * W] = result[a * M : (a + 1) * M]

        for c in range(S):
            i = h * S + c

            @pl.when(place + 1 < plan.line)
            def _():
                out_copy(p, i, up, p + 2).start()

            @pl.when(place >= 1)
            def _():
                out_copy(p, i, down, p - 2).start()

            out_copy(p, i, partner, mate).start()

        return carry

    lax.fori_loop(0, G, group_step, 0)

    for k in range(1, plan.line):
        def forward_step(i, carry):
            @pl.when(place >= k)
            def _():
                piece = p - 2 * k
                out_copy(piece, i, up, mate).wait_recv()

                @pl.when(place + 1 < plan.line)
                def _():
                    out_copy(piece, i, up, p + 2).start()

                @pl.when((piece != paired) | (lax.rem(i, 2) == 0))
                def _():
                    out_copy(piece, i, partner, mate).start()

            @pl.when(place + k < plan.line)
            def _():
                piece = p + 2 * k
                out_copy(piece, i, down, mate).wait_recv()

                @pl.when(place >= 1)
                def _():
                    out_copy(piece, i, down, p - 2).start()

                @pl.when((piece != paired) | (lax.rem(i, 2) == 0))
                def _():
                    out_copy(piece, i, partner, mate).start()

            if k == 1:
                @pl.when(lax.rem(i, 2) == 1)
                def _():
                    out_copy(mate, i, across, mate).wait_recv()
                    out_copy(mate, i, across, paired).start()

            return carry

        lax.fori_loop(0, G * S, forward_step, 0)

    modes = plan.line * own

    def side_part(b, a):
        columns = pl.ds(pl.multiple_of(a * W, W), W)
        block = out[b, :, :, :, columns].reshape(modes, W).T
        return dot(block, turned[b])

    def first_side(a, carry):
        total[pl.ds(pl.multiple_of(a * W, W), W)] = side_part(side, a)
        return carry

    lax.fori_loop(0, C, first_side, 0)

    def sag_copy(a):
        rows = pl.ds(pl.multiple_of(a * W, W), W)
        return pltpu.make_async_copy(rounded.at[rows], sag.at[rows], sag_sem.at[a])

    def second_side(c, carry):
        for z in range(plan.line):
            for h in range(G):
                i = h * S + c

                @pl.when((z != place) | (c == 0))
                def _():
                    out_copy(2 * z + 1 - side, i, partner, mate).wait_recv()

        def step(j, inner):
            a = c * (C // S) + j
            rows = pl.ds(pl.multiple_of(a * W, W), W)
            rounded[rows] = (total[rows] + side_part(1 - side, a)).astype(BF16)
            sag_copy(a).start()
            return inner

        lax.fori_loop(0, C // S, step, 0)
        return carry

    lax.fori_loop(0, S, second_side, 0)

    def finish(n, carry):
        i = lax.rem(n, G * S)
        z = n // (G * S)
        piece = 2 * z + side

        @pl.when((z != pair) | (lax.rem(i, 2) == 0))
        def _():
            out_copy(piece, i, partner, mate).wait_send()

        @pl.when((z == place) & (lax.rem(i, 2) == 1))
        def _():
            out_copy(mate, i, across, mate).wait_send()

        @pl.when((z <= place) & (place + 1 < plan.line))
        def _():
            out_copy(piece, i, up, mate).wait_send()

        @pl.when((z >= place) & (place >= 1))
        def _():
            out_copy(piece, i, down, mate).wait_send()

        return carry

    lax.fori_loop(0, plan.line * G * S, finish, 0)
    for a in range(C):
        sag_copy(a).wait()
    for k in range(1, N):
        part_copy(k).wait_send()
    for k in range(1, plan.ways):
        merged_copy(k).wait_send()
    for d in range(1, R + 1):
        @pl.when(t + d < T)
        def _():
            for h in range(G):
                modal_copy(d, h).wait_send()


def sag_call(plan, counters, signatures, eigen, taps, forward, inverse):
    T, N, W, C, R, own = plan.tm, plan.port, plan.width, plan.blocks, plan.reach, plan.own
    G, M, S = plan.groups, plan.group, plan.pieces
    dma = pltpu.SemaphoreType.DMA
    return pl.pallas_call(
        functools.partial(sag_kernel, plan),
        out_shape=jax.ShapeDtypeStruct((plan.cycles, plan.ports), BF16),
        in_specs=[pl.BlockSpec(memory_space=pl.ANY)] * 6,
        out_specs=pl.BlockSpec(memory_space=pl.ANY),
        scratch_shapes=[
            pltpu.VMEM(counters.shape, BF16),
            pltpu.VMEM(signatures.shape, BF16),
            pltpu.VMEM(eigen.shape, BF16),
            pltpu.VMEM(taps.shape, BF16),
            pltpu.VMEM(forward.shape, BF16),
            pltpu.VMEM(inverse.shape, BF16),
            pltpu.VMEM((N * own, plan.tallies), F32),
            pltpu.VMEM((N, plan.rows, plan.tallies), F32),
            pltpu.VMEM((plan.ways, plan.rows, plan.tallies), F32),
            pltpu.VMEM((R + 1, G, M, plan.cycles), BF16),
            pltpu.VMEM(((R + 1) * C, M, 2 * W), F32),
            pltpu.VMEM((plan.lags, own, 2 * W), F32),
            pltpu.VMEM((C, M, 2 * W), F32),
            pltpu.VMEM((2, plan.line, G, M, plan.cycles), BF16),
            pltpu.VMEM((2, plan.line * own, plan.ports), BF16),
            pltpu.VMEM((plan.cycles, plan.ports), F32),
            pltpu.VMEM((plan.cycles, plan.ports), BF16),
            dma((6,)), dma((N,)), dma((N,)), dma((plan.ways,)), dma((plan.ways,)),
            dma((R + 1, G)), dma((R + 1, G)), dma((N, G * S, 4)), dma((N, G * S)), dma((C,)),
        ],
        compiler_params=pltpu.CompilerParams(
            collective_id=0, has_side_effects=True, vmem_limit_bytes=LARGE_GRANT
        ),
        name="sag",
    )(counters, signatures, eigen, taps, forward, inverse)


def solution(mesh):
    def per_device(counters, signatures, eigen, taps):
        plan = Plan(
            mesh.shape["tm"], mesh.shape["port"], counters.shape[0], eigen.shape[0],
            counters.shape[1], taps.shape[0], taps.shape[1],
        )
        forward, inverse = odd_dft(plan.width)
        return sag_call(
            plan, counters, signatures, eigen, taps, jnp.asarray(forward), jnp.asarray(inverse)
        )

    in_specs = (P("tm", None), P(None, "port"), P("port", None), P("port", None))
    return jax.shard_map(
        per_device, mesh=mesh, in_specs=in_specs, out_specs=P("tm", "port"), check_vma=False
    )
```

```python
import functools

import jax
import jax.numpy as jnp
import ml_dtypes
import numpy as np
from jax import lax
from jax.experimental import pallas as pl
from jax.experimental.pallas import tpu as pltpu
from jax.sharding import PartitionSpec as P

MESH = pl.DeviceIdType.MESH
LARGE_GRANT = 60 * 1024 * 1024
F32 = jnp.float32
BF16 = jnp.bfloat16
NT = (((1,), (1,)), ((), ()))
TN = (((0,), (0,)), ((), ()))


def split_parts(x):
    high = x.astype(ml_dtypes.bfloat16)
    low = (x - high.astype(np.float64)).astype(ml_dtypes.bfloat16)
    return high, low


def odd_dft(width):
    theta = np.pi * (2 * np.arange(width) + 1) / (2 * width)
    phase = np.outer(np.arange(width), theta)
    forward = np.concatenate([np.cos(phase), -np.sin(phase)], axis=1)
    phase = np.outer(theta, width + np.arange(width))
    inverse = np.concatenate([np.cos(phase), -np.sin(phase)], axis=0) / width
    return np.concatenate(split_parts(forward), axis=0), np.concatenate(split_parts(inverse), axis=0)


def halves(x):
    high = x.astype(BF16)
    return high, (x - high.astype(F32)).astype(BF16)


def dot(a, b):
    return jnp.dot(a, b, preferred_element_type=F32)


class Plan:
    def __init__(self, tm, port, cycles, ports, tallies, own, span):
        self.tm, self.port, self.cycles, self.ports, self.tallies = tm, port, cycles, ports, tallies
        self.own, self.span = own, span
        self.width = min(256, cycles)
        self.blocks = cycles // self.width
        self.lags = span // self.width
        self.reach = min((span - 2) // cycles + 1, tm - 1)
        self.ways = min(tm, own // 8)
        self.rows = own // self.ways
        self.line = port // 2
        self.group = min(16, own)
        self.groups = own // self.group
        self.pieces = 2
        self.strips = 8


def sag_kernel(
    plan, counters, signatures, eigen, taps, forward, inverse, sag,
    cnt, sig, eig, tap, fwd, inv, partial, parts, merged, xs, spectra, taps_spectra, product, out, turned, total, rounded,
    load_sem, part_send, part_recv, merged_send, merged_recv, modal_send, modal_recv, out_send, out_recv, sag_sem,
):
    T, N, W, C, R, own = plan.tm, plan.port, plan.width, plan.blocks, plan.reach, plan.own
    G, M = plan.groups, plan.group
    t, p = lax.axis_index("tm"), lax.axis_index("port")
    loads = [
        pltpu.make_async_copy(src, dst, load_sem.at[i])
        for i, (src, dst) in enumerate(
            [(signatures, sig), (eigen, eig), (forward, fwd), (taps, tap), (counters, cnt), (inverse, inv)]
        )
    ]
    for load in loads:
        load.start()

    barrier = pltpu.get_barrier_semaphore()
    for k in range(1, N):
        pl.semaphore_signal(
            barrier, inc=1, device_id={"tm": t, "port": lax.rem(p + k, N)}, device_id_type=MESH
        )
    greeted = N - 1
    for k in range(1, R + 1):
        @pl.when(t + k < T)
        def _():
            pl.semaphore_signal(barrier, inc=1, device_id={"tm": t + k, "port": p}, device_id_type=MESH)

        @pl.when(t - k >= 0)
        def _():
            pl.semaphore_signal(barrier, inc=1, device_id={"tm": t - k, "port": p}, device_id_type=MESH)

        greeted = greeted + jnp.where(t + k < T, 1, 0) + jnp.where(t - k >= 0, 1, 0)

    loads[0].wait()
    loads[1].wait()
    partial[...] = dot(sig[...], eig[...]).T
    pl.semaphore_wait(barrier, greeted)

    share = lax.rem(t, plan.ways)

    def part_copy(k):
        to = lax.rem(p + k, N)
        return pltpu.make_async_remote_copy(
            src_ref=partial.at[pl.ds(pl.multiple_of(to * own + share * plan.rows, 8), plan.rows)],
            dst_ref=parts.at[k],
            send_sem=part_send.at[k],
            recv_sem=part_recv.at[k],
            device_id={"tm": t, "port": to},
            device_id_type=MESH,
        )

    for k in range(1, N):
        part_copy(k).start()

    loads[2].wait()
    loads[3].wait()

    def transform(x):
        return dot(x, fwd[:W]) + dot(x, fwd[W:])

    quad = 4

    def taps_step(i, carry):
        rows = [tap[:, pl.ds(pl.multiple_of((i * quad + j) * W, W), W)] for j in range(quad)]
        result = transform(jnp.concatenate(rows, axis=0))
        taps_spectra[pl.ds(i * quad, quad)] = result.reshape(quad, own, 2 * W)
        return carry

    lax.fori_loop(0, plan.lags // quad, taps_step, 0)
    tile = min(256, plan.ports)
    for i in range(plan.ports // tile):
        block = eig[i * tile : (i + 1) * tile].T
        for piece in range(N):
            z, b = divmod(piece, 2)
            turned[b, z * own : (z + 1) * own, i * tile : (i + 1) * tile] = block[piece * own : (piece + 1) * own]
    for d in range(1, R + 1):
        @pl.when(t < d)
        def _():
            xs[d] = jnp.zeros_like(xs[d])

    octet = partial[pl.ds(pl.multiple_of(p * own + share * plan.rows, 8), plan.rows)]
    for k in range(1, N):
        part_copy(k).wait_recv()
        octet = octet + parts[k]
    merged[share] = octet

    def merged_copy(k):
        mate = t - share + lax.rem(share + k, plan.ways)
        return pltpu.make_async_remote_copy(
            src_ref=merged.at[share],
            dst_ref=merged.at[share],
            send_sem=merged_send.at[k],
            recv_sem=merged_recv.at[k],
            device_id={"tm": mate, "port": p},
            device_id_type=MESH,
        )

    for k in range(1, plan.ways):
        merged_copy(k).start()
    loads[4].wait()
    for k in range(1, plan.ways):
        came = lax.rem(share + plan.ways - k, plan.ways)
        pltpu.make_async_remote_copy(
            src_ref=merged.at[came], dst_ref=merged.at[came], send_sem=merged_send.at[k],
            recv_sem=merged_recv.at[k], device_id={"tm": t - share + came, "port": p}, device_id_type=MESH,
        ).wait_recv()

    high, low = halves(merged[...].reshape(own, plan.tallies))
    both = lax.dot_general(jnp.concatenate([high, low], axis=0), cnt[...], NT, preferred_element_type=F32)
    modal = (both[:own] + both[own:]).astype(BF16)
    xs[0] = modal.reshape(G, M, plan.cycles)

    def modal_copy(d, h):
        return pltpu.make_async_remote_copy(
            src_ref=xs.at[0, h],
            dst_ref=xs.at[d, h],
            send_sem=modal_send.at[d, h],
            recv_sem=modal_recv.at[d, h],
            device_id={"tm": t + d, "port": p},
            device_id_type=MESH,
        )

    for h in range(G):
        for d in range(1, R + 1):
            @pl.when(t + d < T)
            def _():
                modal_copy(d, h).start()

    sign = 1.0 - 2.0 * (lax.broadcasted_iota(jnp.int32, (8, 128), 1) % 2).astype(F32)

    def product_step(h, g):
        rows = pl.ds(pl.multiple_of(g * 8, 8), 8)
        taps_rows = pl.ds(pl.multiple_of(h * M + g * 8, 8), 8)
        for q in range(W // 128):
            re, im = slice(q * 128, q * 128 + 128), slice(W + q * 128, W + q * 128 + 128)
            acc_re, acc_im = [None] * C, [None] * C
            before = None
            for j in range(-R * C, C):
                now = (spectra[R * C + j, rows, re], spectra[R * C + j, rows, im])
                z_re, z_im = sign * now[1], -(sign * now[0])
                if before is not None:
                    z_re, z_im = z_re + before[0], z_im + before[1]
                before = now
                for a in range(C):
                    lag = a - j
                    if 0 <= lag < plan.lags:
                        h_re, h_im = taps_spectra[lag, taps_rows, re], taps_spectra[lag, taps_rows, im]
                        add_re, add_im = h_re * z_re - h_im * z_im, h_re * z_im + h_im * z_re
                        acc_re[a] = add_re if acc_re[a] is None else acc_re[a] + add_re
                        acc_im[a] = add_im if acc_im[a] is None else acc_im[a] + add_im
            for a in range(C):
                product[a, rows, re] = acc_re[a]
                product[a, rows, im] = acc_im[a]

    place, side = p // 2, lax.rem(p, 2)
    S = plan.pieces
    wide = plan.cycles // S
    up, down, partner, across = 0, 1, 2, 3
    mate = p + 1 - 2 * side
    pair = place + 1 - 2 * lax.rem(place, 2)
    paired = 2 * pair + side

    def out_copy(piece, i, way, to):
        h = i // S
        c = lax.rem(i, S)
        part = out.at[lax.rem(piece, 2), piece // 2, h, :, pl.ds(pl.multiple_of(c * wide, wide), wide)]
        return pltpu.make_async_remote_copy(
            src_ref=part,
            dst_ref=part,
            send_sem=out_send.at[piece, i, way],
            recv_sem=out_recv.at[piece, i],
            device_id={"tm": t, "port": to},
            device_id_type=MESH,
        )

    loads[5].wait()

    def group_step(h, carry):
        for d in range(1, R + 1):
            @pl.when(t >= d)
            def _():
                modal_copy(d, h).wait_recv()

        rows = [
            xs[d, h, :, i * W : (i + 1) * W] for d in range(R, -1, -1) for i in range(C)
        ]
        spectra[...] = transform(jnp.concatenate(rows, axis=0)).reshape((R + 1) * C, M, 2 * W)

        def step(g, inner):
            product_step(h, g)
            return inner

        lax.fori_loop(0, M // 8, step, 0)
        high, low = halves(product[...].reshape(C * M, 2 * W))
        result = dot(high, inv[: 2 * W]) + dot(low, inv[: 2 * W]) + dot(high, inv[2 * W :])
        result = result.astype(BF16)
        for a in range(C):
            out[side, place, h, :, a * W : (a + 1) * W] = result[a * M : (a + 1) * M]

        for c in range(S):
            i = h * S + c

            @pl.when(place + 1 < plan.line)
            def _():
                out_copy(p, i, up, p + 2).start()

            @pl.when(place >= 1)
            def _():
                out_copy(p, i, down, p - 2).start()

            out_copy(p, i, partner, mate).start()

        return carry

    lax.fori_loop(0, G, group_step, 0)

    for k in range(1, plan.line):
        def forward_step(i, carry):
            @pl.when(place >= k)
            def _():
                piece = p - 2 * k
                out_copy(piece, i, up, mate).wait_recv()

                @pl.when(place + 1 < plan.line)
                def _():
                    out_copy(piece, i, up, p + 2).start()

                @pl.when((piece != paired) | (lax.rem(i, 2) == 0))
                def _():
                    out_copy(piece, i, partner, mate).start()

            @pl.when(place + k < plan.line)
            def _():
                piece = p + 2 * k
                out_copy(piece, i, down, mate).wait_recv()

                @pl.when(place >= 1)
                def _():
                    out_copy(piece, i, down, p - 2).start()

                @pl.when((piece != paired) | (lax.rem(i, 2) == 0))
                def _():
                    out_copy(piece, i, partner, mate).start()

            if k == 1:
                @pl.when(lax.rem(i, 2) == 1)
                def _():
                    out_copy(mate, i, across, mate).wait_recv()
                    out_copy(mate, i, across, paired).start()

            return carry

        lax.fori_loop(0, G * S, forward_step, 0)

    modes = plan.line * own

    def side_part(b, a):
        columns = pl.ds(pl.multiple_of(a * W, W), W)
        block = out[b, :, :, :, columns].reshape(modes, W).T
        return dot(block, turned[b])

    def first_side(a, carry):
        total[pl.ds(pl.multiple_of(a * W, W), W)] = side_part(side, a)
        return carry

    lax.fori_loop(0, C, first_side, 0)

    def sag_copy(a):
        rows = pl.ds(pl.multiple_of(a * W, W), W)
        return pltpu.make_async_copy(rounded.at[rows], sag.at[rows], sag_sem.at[a])

    def second_side(c, carry):
        for z in range(plan.line):
            for h in range(G):
                i = h * S + c

                @pl.when((z != place) | (c == 0))
                def _():
                    out_copy(2 * z + 1 - side, i, partner, mate).wait_recv()

        def step(j, inner):
            a = c * (C // S) + j
            rows = pl.ds(pl.multiple_of(a * W, W), W)
            rounded[rows] = (total[rows] + side_part(1 - side, a)).astype(BF16)
            sag_copy(a).start()
            return inner

        lax.fori_loop(0, C // S, step, 0)
        return carry

    lax.fori_loop(0, S, second_side, 0)

    def finish(n, carry):
        i = lax.rem(n, G * S)
        z = n // (G * S)
        piece = 2 * z + side

        @pl.when((z != pair) | (lax.rem(i, 2) == 0))
        def _():
            out_copy(piece, i, partner, mate).wait_send()

        @pl.when((z == place) & (lax.rem(i, 2) == 1))
        def _():
            out_copy(mate, i, across, mate).wait_send()

        @pl.when((z <= place) & (place + 1 < plan.line))
        def _():
            out_copy(piece, i, up, mate).wait_send()

        @pl.when((z >= place) & (place >= 1))
        def _():
            out_copy(piece, i, down, mate).wait_send()

        return carry

    lax.fori_loop(0, plan.line * G * S, finish, 0)
    for a in range(C):
        sag_copy(a).wait()
    for k in range(1, N):
        part_copy(k).wait_send()
    for k in range(1, plan.ways):
        merged_copy(k).wait_send()
    for d in range(1, R + 1):
        @pl.when(t + d < T)
        def _():
            for h in range(G):
                modal_copy(d, h).wait_send()


def sag_call(plan, counters, signatures, eigen, taps, forward, inverse):
    T, N, W, C, R, own = plan.tm, plan.port, plan.width, plan.blocks, plan.reach, plan.own
    G, M, S = plan.groups, plan.group, plan.pieces
    dma = pltpu.SemaphoreType.DMA
    return pl.pallas_call(
        functools.partial(sag_kernel, plan),
        out_shape=jax.ShapeDtypeStruct((plan.cycles, plan.ports), BF16),
        in_specs=[pl.BlockSpec(memory_space=pl.ANY)] * 6,
        out_specs=pl.BlockSpec(memory_space=pl.ANY),
        scratch_shapes=[
            pltpu.VMEM(counters.shape, BF16),
            pltpu.VMEM(signatures.shape, BF16),
            pltpu.VMEM(eigen.shape, BF16),
            pltpu.VMEM(taps.shape, BF16),
            pltpu.VMEM(forward.shape, BF16),
            pltpu.VMEM(inverse.shape, BF16),
            pltpu.VMEM((N * own, plan.tallies), F32),
            pltpu.VMEM((N, plan.rows, plan.tallies), F32),
            pltpu.VMEM((plan.ways, plan.rows, plan.tallies), F32),
            pltpu.VMEM((R + 1, G, M, plan.cycles), BF16),
            pltpu.VMEM(((R + 1) * C, M, 2 * W), F32),
            pltpu.VMEM((plan.lags, own, 2 * W), F32),
            pltpu.VMEM((C, M, 2 * W), F32),
            pltpu.VMEM((2, plan.line, G, M, plan.cycles), BF16),
            pltpu.VMEM((2, plan.line * own, plan.ports), BF16),
            pltpu.VMEM((plan.cycles, plan.ports), F32),
            pltpu.VMEM((plan.cycles, plan.ports), BF16),
            dma((6,)), dma((N,)), dma((N,)), dma((plan.ways,)), dma((plan.ways,)),
            dma((R + 1, G)), dma((R + 1, G)), dma((N, G * S, 4)), dma((N, G * S)), dma((C,)),
        ],
        compiler_params=pltpu.CompilerParams(
            collective_id=0, has_side_effects=True, vmem_limit_bytes=LARGE_GRANT
        ),
        name="sag",
    )(counters, signatures, eigen, taps, forward, inverse)


def placed_kernel(plan, source, target, sem):
    rows = plan.cycles // plan.strips
    copies = [
        pltpu.make_async_copy(
            source.at[pl.ds(i * rows, rows)], target.at[pl.ds(i * rows, rows)], sem.at[i]
        )
        for i in range(plan.strips)
    ]
    for copy in copies:
        copy.start()
    for copy in copies:
        copy.wait()


def placed(plan, sag):
    return pl.pallas_call(
        functools.partial(placed_kernel, plan),
        out_shape=jax.ShapeDtypeStruct(sag.shape, sag.dtype),
        in_specs=[pl.BlockSpec(memory_space=pl.ANY)],
        out_specs=pl.BlockSpec(memory_space=pl.ANY),
        scratch_shapes=[pltpu.SemaphoreType.DMA((plan.strips,))],
        compiler_params=pltpu.CompilerParams(vmem_limit_bytes=LARGE_GRANT),
        name="placed",
    )(sag)


def solution(mesh):
    def per_device(counters, signatures, eigen, taps):
        plan = Plan(
            mesh.shape["tm"], mesh.shape["port"], counters.shape[0], eigen.shape[0],
            counters.shape[1], taps.shape[0], taps.shape[1],
        )
        forward, inverse = odd_dft(plan.width)
        sag = sag_call(
            plan, counters, signatures, eigen, taps, jnp.asarray(forward), jnp.asarray(inverse)
        )
        return placed(plan, sag)

    in_specs = (P("tm", None), P(None, "port"), P("port", None), P("port", None))
    return jax.shard_map(
        per_device, mesh=mesh, in_specs=in_specs, out_specs=P("tm", "port"), check_vma=False
    )
```

```python
import functools

import jax
import jax.numpy as jnp
import ml_dtypes
import numpy as np
from jax import lax
from jax.experimental import pallas as pl
from jax.experimental.pallas import tpu as pltpu
from jax.sharding import PartitionSpec as P

MESH = pl.DeviceIdType.MESH
LARGE_GRANT = 60 * 1024 * 1024
F32 = jnp.float32
BF16 = jnp.bfloat16
NT = (((1,), (1,)), ((), ()))
TN = (((0,), (0,)), ((), ()))


def split_parts(x):
    high = x.astype(ml_dtypes.bfloat16)
    low = (x - high.astype(np.float64)).astype(ml_dtypes.bfloat16)
    return high, low


def odd_dft(width):
    theta = np.pi * (2 * np.arange(width) + 1) / (2 * width)
    phase = np.outer(np.arange(width), theta)
    forward = np.concatenate([np.cos(phase), -np.sin(phase)], axis=1)
    phase = np.outer(theta, width + np.arange(width))
    inverse = np.concatenate([np.cos(phase), -np.sin(phase)], axis=0) / width
    return np.concatenate(split_parts(forward), axis=0), np.concatenate(split_parts(inverse), axis=0)


def halves(x):
    high = x.astype(BF16)
    return high, (x - high.astype(F32)).astype(BF16)


def dot(a, b):
    return jnp.dot(a, b, preferred_element_type=F32)


class Plan:
    def __init__(self, tm, port, cycles, ports, tallies, own, span):
        self.tm, self.port, self.cycles, self.ports, self.tallies = tm, port, cycles, ports, tallies
        self.own, self.span = own, span
        self.width = min(256, cycles)
        self.blocks = cycles // self.width
        self.lags = span // self.width
        self.reach = min((span - 2) // cycles + 1, tm - 1)
        self.ways = min(tm, own // 8)
        self.rows = own // self.ways
        self.line = port // 2
        self.group = min(16, own)
        self.groups = own // self.group
        self.pieces = 2
        self.strips = 8


def sag_kernel(
    plan, counters, signatures, eigen, taps, forward, inverse, sag,
    cnt, sig, eig, tap, fwd, inv, partial, parts, merged, xs, spectra, taps_spectra, product, out, turned, total, rounded,
    load_sem, part_send, part_recv, merged_send, merged_recv, modal_send, modal_recv, out_send, out_recv, sag_sem,
):
    T, N, W, C, R, own = plan.tm, plan.port, plan.width, plan.blocks, plan.reach, plan.own
    G, M = plan.groups, plan.group
    t, p = lax.axis_index("tm"), lax.axis_index("port")
    loads = [
        pltpu.make_async_copy(src, dst, load_sem.at[i])
        for i, (src, dst) in enumerate(
            [(signatures, sig), (eigen, eig), (forward, fwd), (taps, tap), (counters, cnt), (inverse, inv)]
        )
    ]
    for load in loads:
        load.start()

    barrier = pltpu.get_barrier_semaphore()
    for k in range(1, N):
        pl.semaphore_signal(
            barrier, inc=1, device_id={"tm": t, "port": lax.rem(p + k, N)}, device_id_type=MESH
        )
    greeted = N - 1
    for k in range(1, R + 1):
        @pl.when(t + k < T)
        def _():
            pl.semaphore_signal(barrier, inc=1, device_id={"tm": t + k, "port": p}, device_id_type=MESH)

        @pl.when(t - k >= 0)
        def _():
            pl.semaphore_signal(barrier, inc=1, device_id={"tm": t - k, "port": p}, device_id_type=MESH)

        greeted = greeted + jnp.where(t + k < T, 1, 0) + jnp.where(t - k >= 0, 1, 0)

    loads[0].wait()
    loads[1].wait()
    partial[...] = dot(sig[...], eig[...]).T
    pl.semaphore_wait(barrier, greeted)

    share = lax.rem(t, plan.ways)

    def part_copy(k):
        to = lax.rem(p + k, N)
        return pltpu.make_async_remote_copy(
            src_ref=partial.at[pl.ds(pl.multiple_of(to * own + share * plan.rows, 8), plan.rows)],
            dst_ref=parts.at[k],
            send_sem=part_send.at[k],
            recv_sem=part_recv.at[k],
            device_id={"tm": t, "port": to},
            device_id_type=MESH,
        )

    for k in range(1, N):
        part_copy(k).start()

    loads[2].wait()
    loads[3].wait()

    def transform(x):
        return dot(x, fwd[:W]) + dot(x, fwd[W:])

    quad = 4

    def taps_step(i, carry):
        rows = [tap[:, pl.ds(pl.multiple_of((i * quad + j) * W, W), W)] for j in range(quad)]
        result = transform(jnp.concatenate(rows, axis=0))
        taps_spectra[pl.ds(i * quad, quad)] = result.reshape(quad, own, 2 * W)
        return carry

    lax.fori_loop(0, plan.lags // quad, taps_step, 0)
    tile = min(256, plan.ports)
    for i in range(plan.ports // tile):
        block = eig[i * tile : (i + 1) * tile].T
        for piece in range(N):
            z, b = divmod(piece, 2)
            turned[b, z * own : (z + 1) * own, i * tile : (i + 1) * tile] = block[piece * own : (piece + 1) * own]
    for d in range(1, R + 1):
        @pl.when(t < d)
        def _():
            xs[d] = jnp.zeros_like(xs[d])

    octet = partial[pl.ds(pl.multiple_of(p * own + share * plan.rows, 8), plan.rows)]
    for k in range(1, N):
        part_copy(k).wait_recv()
        octet = octet + parts[k]
    merged[share] = octet

    def merged_copy(k):
        mate = t - share + lax.rem(share + k, plan.ways)
        return pltpu.make_async_remote_copy(
            src_ref=merged.at[share],
            dst_ref=merged.at[share],
            send_sem=merged_send.at[k],
            recv_sem=merged_recv.at[k],
            device_id={"tm": mate, "port": p},
            device_id_type=MESH,
        )

    for k in range(1, plan.ways):
        merged_copy(k).start()
    loads[4].wait()
    for k in range(1, plan.ways):
        came = lax.rem(share + plan.ways - k, plan.ways)
        pltpu.make_async_remote_copy(
            src_ref=merged.at[came], dst_ref=merged.at[came], send_sem=merged_send.at[k],
            recv_sem=merged_recv.at[k], device_id={"tm": t - share + came, "port": p}, device_id_type=MESH,
        ).wait_recv()

    high, low = halves(merged[...].reshape(own, plan.tallies))
    both = lax.dot_general(jnp.concatenate([high, low], axis=0), cnt[...], NT, preferred_element_type=F32)
    modal = (both[:own] + both[own:]).astype(BF16)
    xs[0] = modal.reshape(G, M, plan.cycles)

    def modal_copy(d, h):
        return pltpu.make_async_remote_copy(
            src_ref=xs.at[0, h],
            dst_ref=xs.at[d, h],
            send_sem=modal_send.at[d, h],
            recv_sem=modal_recv.at[d, h],
            device_id={"tm": t + d, "port": p},
            device_id_type=MESH,
        )

    for h in range(G):
        for d in range(1, R + 1):
            @pl.when(t + d < T)
            def _():
                modal_copy(d, h).start()

    sign = 1.0 - 2.0 * (lax.broadcasted_iota(jnp.int32, (8, 128), 1) % 2).astype(F32)

    def product_step(h, g):
        rows = pl.ds(pl.multiple_of(g * 8, 8), 8)
        taps_rows = pl.ds(pl.multiple_of(h * M + g * 8, 8), 8)
        for q in range(W // 128):
            re, im = slice(q * 128, q * 128 + 128), slice(W + q * 128, W + q * 128 + 128)
            acc_re, acc_im = [None] * C, [None] * C
            before = None
            for j in range(-R * C, C):
                now = (spectra[R * C + j, rows, re], spectra[R * C + j, rows, im])
                z_re, z_im = sign * now[1], -(sign * now[0])
                if before is not None:
                    z_re, z_im = z_re + before[0], z_im + before[1]
                before = now
                for a in range(C):
                    lag = a - j
                    if 0 <= lag < plan.lags:
                        h_re, h_im = taps_spectra[lag, taps_rows, re], taps_spectra[lag, taps_rows, im]
                        add_re, add_im = h_re * z_re - h_im * z_im, h_re * z_im + h_im * z_re
                        acc_re[a] = add_re if acc_re[a] is None else acc_re[a] + add_re
                        acc_im[a] = add_im if acc_im[a] is None else acc_im[a] + add_im
            for a in range(C):
                product[a, rows, re] = acc_re[a]
                product[a, rows, im] = acc_im[a]

    place, side = p // 2, lax.rem(p, 2)
    S = plan.pieces
    wide = plan.cycles // S
    up, down, partner, across = 0, 1, 2, 3
    mate = p + 1 - 2 * side
    pair = place + 1 - 2 * lax.rem(place, 2)
    paired = 2 * pair + side

    def out_copy(piece, i, way, to):
        h = i // S
        c = lax.rem(i, S)
        part = out.at[lax.rem(piece, 2), piece // 2, h, :, pl.ds(pl.multiple_of(c * wide, wide), wide)]
        return pltpu.make_async_remote_copy(
            src_ref=part,
            dst_ref=part,
            send_sem=out_send.at[piece, i, way],
            recv_sem=out_recv.at[piece, i],
            device_id={"tm": t, "port": to},
            device_id_type=MESH,
        )

    loads[5].wait()

    def group_step(h, carry):
        for d in range(1, R + 1):
            @pl.when(t >= d)
            def _():
                modal_copy(d, h).wait_recv()

        rows = [
            xs[d, h, :, i * W : (i + 1) * W] for d in range(R, -1, -1) for i in range(C)
        ]
        spectra[...] = transform(jnp.concatenate(rows, axis=0)).reshape((R + 1) * C, M, 2 * W)

        def step(g, inner):
            product_step(h, g)
            return inner

        lax.fori_loop(0, M // 8, step, 0)
        high, low = halves(product[...].reshape(C * M, 2 * W))
        result = dot(high, inv[: 2 * W]) + dot(low, inv[: 2 * W]) + dot(high, inv[2 * W :])
        result = result.astype(BF16)
        for a in range(C):
            out[side, place, h, :, a * W : (a + 1) * W] = result[a * M : (a + 1) * M]

        for c in range(S):
            i = h * S + c

            @pl.when(place + 1 < plan.line)
            def _():
                out_copy(p, i, up, p + 2).start()

            @pl.when(place >= 1)
            def _():
                out_copy(p, i, down, p - 2).start()

            out_copy(p, i, partner, mate).start()

        return carry

    lax.fori_loop(0, G, group_step, 0)

    for k in range(1, plan.line):
        def forward_step(i, carry):
            @pl.when(place >= k)
            def _():
                piece = p - 2 * k
                out_copy(piece, i, up, mate).wait_recv()

                @pl.when(place + 1 < plan.line)
                def _():
                    out_copy(piece, i, up, p + 2).start()

                @pl.when((piece != paired) | (lax.rem(i, 2) == 0))
                def _():
                    out_copy(piece, i, partner, mate).start()

            @pl.when(place + k < plan.line)
            def _():
                piece = p + 2 * k
                out_copy(piece, i, down, mate).wait_recv()

                @pl.when(place >= 1)
                def _():
                    out_copy(piece, i, down, p - 2).start()

                @pl.when((piece != paired) | (lax.rem(i, 2) == 0))
                def _():
                    out_copy(piece, i, partner, mate).start()

            if k == 1:
                @pl.when(lax.rem(i, 2) == 1)
                def _():
                    out_copy(mate, i, across, mate).wait_recv()
                    out_copy(mate, i, across, paired).start()

            return carry

        lax.fori_loop(0, G * S, forward_step, 0)

    modes = plan.line * own

    def side_part(b, a):
        columns = pl.ds(pl.multiple_of(a * W, W), W)
        block = out[b, :, :, :, columns].reshape(modes, W).T
        return dot(block, turned[b])

    def first_side(a, carry):
        total[pl.ds(pl.multiple_of(a * W, W), W)] = side_part(side, a)
        return carry

    lax.fori_loop(0, C, first_side, 0)

    def sag_copy(a):
        rows = pl.ds(pl.multiple_of(a * W, W), W)
        return pltpu.make_async_copy(rounded.at[rows], sag.at[rows], sag_sem.at[a])

    def second_side(c, carry):
        for z in range(plan.line):
            for h in range(G):
                i = h * S + c

                @pl.when((z != place) | (c == 0))
                def _():
                    out_copy(2 * z + 1 - side, i, partner, mate).wait_recv()

        def step(j, inner):
            a = c * (C // S) + j
            rows = pl.ds(pl.multiple_of(a * W, W), W)
            rounded[rows] = (total[rows] + side_part(1 - side, a)).astype(BF16)
            sag_copy(a).start()
            return inner

        lax.fori_loop(0, C // S, step, 0)
        return carry

    lax.fori_loop(0, S, second_side, 0)

    def finish(n, carry):
        i = lax.rem(n, G * S)
        z = n // (G * S)
        piece = 2 * z + side

        @pl.when((z != pair) | (lax.rem(i, 2) == 0))
        def _():
            out_copy(piece, i, partner, mate).wait_send()

        @pl.when((z == place) & (lax.rem(i, 2) == 1))
        def _():
            out_copy(mate, i, across, mate).wait_send()

        @pl.when((z <= place) & (place + 1 < plan.line))
        def _():
            out_copy(piece, i, up, mate).wait_send()

        @pl.when((z >= place) & (place >= 1))
        def _():
            out_copy(piece, i, down, mate).wait_send()

        return carry

    lax.fori_loop(0, plan.line * G * S, finish, 0)
    for a in range(C):
        sag_copy(a).wait()
    for k in range(1, N):
        part_copy(k).wait_send()
    for k in range(1, plan.ways):
        merged_copy(k).wait_send()
    for d in range(1, R + 1):
        @pl.when(t + d < T)
        def _():
            for h in range(G):
                modal_copy(d, h).wait_send()


def sag_call(plan, counters, signatures, eigen, taps, forward, inverse):
    T, N, W, C, R, own = plan.tm, plan.port, plan.width, plan.blocks, plan.reach, plan.own
    G, M, S = plan.groups, plan.group, plan.pieces
    dma = pltpu.SemaphoreType.DMA
    return pl.pallas_call(
        functools.partial(sag_kernel, plan),
        out_shape=jax.ShapeDtypeStruct((plan.cycles, plan.ports), BF16),
        in_specs=[pl.BlockSpec(memory_space=pl.ANY)] * 6,
        out_specs=pl.BlockSpec(memory_space=pl.ANY),
        scratch_shapes=[
            pltpu.VMEM(counters.shape, BF16),
            pltpu.VMEM(signatures.shape, BF16),
            pltpu.VMEM(eigen.shape, BF16),
            pltpu.VMEM(taps.shape, BF16),
            pltpu.VMEM(forward.shape, BF16),
            pltpu.VMEM(inverse.shape, BF16),
            pltpu.VMEM((N * own, plan.tallies), F32),
            pltpu.VMEM((N, plan.rows, plan.tallies), F32),
            pltpu.VMEM((plan.ways, plan.rows, plan.tallies), F32),
            pltpu.VMEM((R + 1, G, M, plan.cycles), BF16),
            pltpu.VMEM(((R + 1) * C, M, 2 * W), F32),
            pltpu.VMEM((plan.lags, own, 2 * W), F32),
            pltpu.VMEM((C, M, 2 * W), F32),
            pltpu.VMEM((2, plan.line, G, M, plan.cycles), BF16),
            pltpu.VMEM((2, plan.line * own, plan.ports), BF16),
            pltpu.VMEM((plan.cycles, plan.ports), F32),
            pltpu.VMEM((plan.cycles, plan.ports), BF16),
            dma((6,)), dma((N,)), dma((N,)), dma((plan.ways,)), dma((plan.ways,)),
            dma((R + 1, G)), dma((R + 1, G)), dma((N, G * S, 4)), dma((N, G * S)), dma((C,)),
        ],
        compiler_params=pltpu.CompilerParams(
            collective_id=0, has_side_effects=True, vmem_limit_bytes=LARGE_GRANT
        ),
        name="sag",
    )(counters, signatures, eigen, taps, forward, inverse)


def placed_kernel(plan, source, target, held, load_sem, store_sem):
    strips = [pl.ds(i * (plan.cycles // plan.strips), plan.cycles // plan.strips) for i in range(plan.strips)]
    loads = [
        pltpu.make_async_copy(source.at[strip], held.at[strip], load_sem.at[i])
        for i, strip in enumerate(strips)
    ]
    stores = [
        pltpu.make_async_copy(held.at[strip], target.at[strip], store_sem.at[i])
        for i, strip in enumerate(strips)
    ]
    for load in loads:
        load.start()
    for load, store in zip(loads, stores):
        load.wait()
        store.start()
    for store in stores:
        store.wait()


def placed(plan, sag):
    return pl.pallas_call(
        functools.partial(placed_kernel, plan),
        out_shape=jax.ShapeDtypeStruct(sag.shape, sag.dtype),
        in_specs=[pl.BlockSpec(memory_space=pl.ANY)],
        out_specs=pl.BlockSpec(memory_space=pl.ANY),
        scratch_shapes=[
            pltpu.VMEM(sag.shape, sag.dtype),
            pltpu.SemaphoreType.DMA((plan.strips,)),
            pltpu.SemaphoreType.DMA((plan.strips,)),
        ],
        compiler_params=pltpu.CompilerParams(vmem_limit_bytes=LARGE_GRANT),
        name="placed",
    )(sag)


def solution(mesh):
    def per_device(counters, signatures, eigen, taps):
        plan = Plan(
            mesh.shape["tm"], mesh.shape["port"], counters.shape[0], eigen.shape[0],
            counters.shape[1], taps.shape[0], taps.shape[1],
        )
        forward, inverse = odd_dft(plan.width)
        sag = sag_call(
            plan, counters, signatures, eigen, taps, jnp.asarray(forward), jnp.asarray(inverse)
        )
        return placed(plan, sag)

    in_specs = (P("tm", None), P(None, "port"), P("port", None), P("port", None))
    return jax.shard_map(
        per_device, mesh=mesh, in_specs=in_specs, out_specs=P("tm", "port"), check_vma=False
    )
```

```python
import functools

import jax
import jax.numpy as jnp
import ml_dtypes
import numpy as np
from jax import lax
from jax.experimental import pallas as pl
from jax.experimental.pallas import tpu as pltpu
from jax.sharding import PartitionSpec as P

MESH = pl.DeviceIdType.MESH
LARGE_GRANT = 60 * 1024 * 1024
F32 = jnp.float32
BF16 = jnp.bfloat16
NT = (((1,), (1,)), ((), ()))
TN = (((0,), (0,)), ((), ()))


def split_parts(x):
    high = x.astype(ml_dtypes.bfloat16)
    low = (x - high.astype(np.float64)).astype(ml_dtypes.bfloat16)
    return high, low


def odd_dft(width):
    theta = np.pi * (2 * np.arange(width) + 1) / (2 * width)
    phase = np.outer(np.arange(width), theta)
    forward = np.concatenate([np.cos(phase), -np.sin(phase)], axis=1)
    phase = np.outer(theta, width + np.arange(width))
    inverse = np.concatenate([np.cos(phase), -np.sin(phase)], axis=0) / width
    return np.concatenate(split_parts(forward), axis=0), np.concatenate(split_parts(inverse), axis=0)


def halves(x):
    high = x.astype(BF16)
    return high, (x - high.astype(F32)).astype(BF16)


def dot(a, b):
    return jnp.dot(a, b, preferred_element_type=F32)


class Plan:
    def __init__(self, tm, port, cycles, ports, tallies, own, span):
        self.tm, self.port, self.cycles, self.ports, self.tallies = tm, port, cycles, ports, tallies
        self.own, self.span = own, span
        self.width = min(256, cycles)
        self.blocks = cycles // self.width
        self.lags = span // self.width
        self.reach = min((span - 2) // cycles + 1, tm - 1)
        self.ways = min(tm, own // 8)
        self.rows = own // self.ways
        self.line = port // 2
        self.group = min(16, own)
        self.groups = own // self.group
        self.pieces = 2


def response_kernel(
    plan, counters, signatures, eigen, taps, forward, inverse, out, turned_out,
    cnt, sig, eig, tap, fwd, inv, partial, parts, merged, xs, spectra, taps_spectra, product, turned,
    load_sem, part_send, part_recv, merged_send, merged_recv, modal_send, modal_recv, out_send, out_recv, turned_sem,
):
    T, N, W, C, R, own = plan.tm, plan.port, plan.width, plan.blocks, plan.reach, plan.own
    G, M = plan.groups, plan.group
    t, p = lax.axis_index("tm"), lax.axis_index("port")
    loads = [
        pltpu.make_async_copy(src, dst, load_sem.at[i])
        for i, (src, dst) in enumerate(
            [(signatures, sig), (eigen, eig), (forward, fwd), (taps, tap), (counters, cnt), (inverse, inv)]
        )
    ]
    for load in loads:
        load.start()

    barrier = pltpu.get_barrier_semaphore()
    for k in range(1, N):
        pl.semaphore_signal(
            barrier, inc=1, device_id={"tm": t, "port": lax.rem(p + k, N)}, device_id_type=MESH
        )
    greeted = N - 1
    for k in range(1, R + 1):
        @pl.when(t + k < T)
        def _():
            pl.semaphore_signal(barrier, inc=1, device_id={"tm": t + k, "port": p}, device_id_type=MESH)

        @pl.when(t - k >= 0)
        def _():
            pl.semaphore_signal(barrier, inc=1, device_id={"tm": t - k, "port": p}, device_id_type=MESH)

        greeted = greeted + jnp.where(t + k < T, 1, 0) + jnp.where(t - k >= 0, 1, 0)

    loads[0].wait()
    loads[1].wait()
    partial[...] = dot(sig[...], eig[...]).T
    pl.semaphore_wait(barrier, greeted)

    share = lax.rem(t, plan.ways)

    def part_copy(k):
        to = lax.rem(p + k, N)
        return pltpu.make_async_remote_copy(
            src_ref=partial.at[pl.ds(pl.multiple_of(to * own + share * plan.rows, 8), plan.rows)],
            dst_ref=parts.at[k],
            send_sem=part_send.at[k],
            recv_sem=part_recv.at[k],
            device_id={"tm": t, "port": to},
            device_id_type=MESH,
        )

    for k in range(1, N):
        part_copy(k).start()

    loads[2].wait()
    loads[3].wait()

    def transform(x):
        return dot(x, fwd[:W]) + dot(x, fwd[W:])

    quad = 4

    def taps_step(i, carry):
        rows = [tap[:, pl.ds(pl.multiple_of((i * quad + j) * W, W), W)] for j in range(quad)]
        result = transform(jnp.concatenate(rows, axis=0))
        taps_spectra[pl.ds(i * quad, quad)] = result.reshape(quad, own, 2 * W)
        return carry

    lax.fori_loop(0, plan.lags // quad, taps_step, 0)
    tile = min(256, plan.ports)
    for i in range(plan.ports // tile):
        block = eig[i * tile : (i + 1) * tile].T
        for piece in range(N):
            z, b = divmod(piece, 2)
            turned[b, z * own : (z + 1) * own, i * tile : (i + 1) * tile] = block[piece * own : (piece + 1) * own]
    turned_copy = pltpu.make_async_copy(turned, turned_out, turned_sem)
    turned_copy.start()
    for d in range(1, R + 1):
        @pl.when(t < d)
        def _():
            xs[d] = jnp.zeros_like(xs[d])

    octet = partial[pl.ds(pl.multiple_of(p * own + share * plan.rows, 8), plan.rows)]
    for k in range(1, N):
        part_copy(k).wait_recv()
        octet = octet + parts[k]
    merged[share] = octet

    def merged_copy(k):
        mate = t - share + lax.rem(share + k, plan.ways)
        return pltpu.make_async_remote_copy(
            src_ref=merged.at[share],
            dst_ref=merged.at[share],
            send_sem=merged_send.at[k],
            recv_sem=merged_recv.at[k],
            device_id={"tm": mate, "port": p},
            device_id_type=MESH,
        )

    for k in range(1, plan.ways):
        merged_copy(k).start()
    loads[4].wait()
    for k in range(1, plan.ways):
        came = lax.rem(share + plan.ways - k, plan.ways)
        pltpu.make_async_remote_copy(
            src_ref=merged.at[came], dst_ref=merged.at[came], send_sem=merged_send.at[k],
            recv_sem=merged_recv.at[k], device_id={"tm": t - share + came, "port": p}, device_id_type=MESH,
        ).wait_recv()

    high, low = halves(merged[...].reshape(own, plan.tallies))
    both = lax.dot_general(jnp.concatenate([high, low], axis=0), cnt[...], NT, preferred_element_type=F32)
    modal = (both[:own] + both[own:]).astype(BF16)
    xs[0] = modal.reshape(G, M, plan.cycles)

    def modal_copy(d, h):
        return pltpu.make_async_remote_copy(
            src_ref=xs.at[0, h],
            dst_ref=xs.at[d, h],
            send_sem=modal_send.at[d, h],
            recv_sem=modal_recv.at[d, h],
            device_id={"tm": t + d, "port": p},
            device_id_type=MESH,
        )

    for h in range(G):
        for d in range(1, R + 1):
            @pl.when(t + d < T)
            def _():
                modal_copy(d, h).start()

    sign = 1.0 - 2.0 * (lax.broadcasted_iota(jnp.int32, (8, 128), 1) % 2).astype(F32)

    def product_step(h, g):
        rows = pl.ds(pl.multiple_of(g * 8, 8), 8)
        taps_rows = pl.ds(pl.multiple_of(h * M + g * 8, 8), 8)
        for q in range(W // 128):
            re, im = slice(q * 128, q * 128 + 128), slice(W + q * 128, W + q * 128 + 128)
            acc_re, acc_im = [None] * C, [None] * C
            before = None
            for j in range(-R * C, C):
                now = (spectra[R * C + j, rows, re], spectra[R * C + j, rows, im])
                z_re, z_im = sign * now[1], -(sign * now[0])
                if before is not None:
                    z_re, z_im = z_re + before[0], z_im + before[1]
                before = now
                for a in range(C):
                    lag = a - j
                    if 0 <= lag < plan.lags:
                        h_re, h_im = taps_spectra[lag, taps_rows, re], taps_spectra[lag, taps_rows, im]
                        add_re, add_im = h_re * z_re - h_im * z_im, h_re * z_im + h_im * z_re
                        acc_re[a] = add_re if acc_re[a] is None else acc_re[a] + add_re
                        acc_im[a] = add_im if acc_im[a] is None else acc_im[a] + add_im
            for a in range(C):
                product[a, rows, re] = acc_re[a]
                product[a, rows, im] = acc_im[a]

    place, side = p // 2, lax.rem(p, 2)
    S = plan.pieces
    wide = plan.cycles // S
    up, down, partner, across = 0, 1, 2, 3
    mate = p + 1 - 2 * side
    pair = place + 1 - 2 * lax.rem(place, 2)
    paired = 2 * pair + side

    def out_copy(piece, i, way, to):
        h = i // S
        c = lax.rem(i, S)
        part = out.at[lax.rem(piece, 2), piece // 2, h, :, pl.ds(pl.multiple_of(c * wide, wide), wide)]
        return pltpu.make_async_remote_copy(
            src_ref=part,
            dst_ref=part,
            send_sem=out_send.at[piece, i, way],
            recv_sem=out_recv.at[piece, i],
            device_id={"tm": t, "port": to},
            device_id_type=MESH,
        )

    loads[5].wait()

    def group_step(h, carry):
        for d in range(1, R + 1):
            @pl.when(t >= d)
            def _():
                modal_copy(d, h).wait_recv()

        rows = [
            xs[d, h, :, i * W : (i + 1) * W] for d in range(R, -1, -1) for i in range(C)
        ]
        spectra[...] = transform(jnp.concatenate(rows, axis=0)).reshape((R + 1) * C, M, 2 * W)

        def step(g, inner):
            product_step(h, g)
            return inner

        lax.fori_loop(0, M // 8, step, 0)
        high, low = halves(product[...].reshape(C * M, 2 * W))
        result = dot(high, inv[: 2 * W]) + dot(low, inv[: 2 * W]) + dot(high, inv[2 * W :])
        result = result.astype(BF16)
        for a in range(C):
            out[side, place, h, :, a * W : (a + 1) * W] = result[a * M : (a + 1) * M]

        for c in range(S):
            i = h * S + c

            @pl.when(place + 1 < plan.line)
            def _():
                out_copy(p, i, up, p + 2).start()

            @pl.when(place >= 1)
            def _():
                out_copy(p, i, down, p - 2).start()

            out_copy(p, i, partner, mate).start()

        return carry

    lax.fori_loop(0, G, group_step, 0)

    for k in range(1, plan.line):
        def forward_step(i, carry):
            @pl.when(place >= k)
            def _():
                piece = p - 2 * k
                out_copy(piece, i, up, mate).wait_recv()

                @pl.when(place + 1 < plan.line)
                def _():
                    out_copy(piece, i, up, p + 2).start()

                @pl.when((piece != paired) | (lax.rem(i, 2) == 0))
                def _():
                    out_copy(piece, i, partner, mate).start()

            @pl.when(place + k < plan.line)
            def _():
                piece = p + 2 * k
                out_copy(piece, i, down, mate).wait_recv()

                @pl.when(place >= 1)
                def _():
                    out_copy(piece, i, down, p - 2).start()

                @pl.when((piece != paired) | (lax.rem(i, 2) == 0))
                def _():
                    out_copy(piece, i, partner, mate).start()

            if k == 1:
                @pl.when(lax.rem(i, 2) == 1)
                def _():
                    out_copy(mate, i, across, mate).wait_recv()
                    out_copy(mate, i, across, paired).start()

            return carry

        lax.fori_loop(0, G * S, forward_step, 0)

    def arrived(n, carry):
        i = lax.rem(n, G * S)
        z = n // (G * S)

        @pl.when((z != place) | (lax.rem(i, 2) == 0))
        def _():
            out_copy(2 * z + 1 - side, i, partner, mate).wait_recv()

        return carry

    lax.fori_loop(0, plan.line * G * S, arrived, 0)

    def finish(n, carry):
        i = lax.rem(n, G * S)
        z = n // (G * S)
        piece = 2 * z + side

        @pl.when((z != pair) | (lax.rem(i, 2) == 0))
        def _():
            out_copy(piece, i, partner, mate).wait_send()

        @pl.when((z == place) & (lax.rem(i, 2) == 1))
        def _():
            out_copy(mate, i, across, mate).wait_send()

        @pl.when((z <= place) & (place + 1 < plan.line))
        def _():
            out_copy(piece, i, up, mate).wait_send()

        @pl.when((z >= place) & (place >= 1))
        def _():
            out_copy(piece, i, down, mate).wait_send()

        return carry

    lax.fori_loop(0, plan.line * G * S, finish, 0)
    turned_copy.wait()
    for k in range(1, N):
        part_copy(k).wait_send()
    for k in range(1, plan.ways):
        merged_copy(k).wait_send()
    for d in range(1, R + 1):
        @pl.when(t + d < T)
        def _():
            for h in range(G):
                modal_copy(d, h).wait_send()


def response_call(plan, counters, signatures, eigen, taps, forward, inverse):
    T, N, W, C, R, own = plan.tm, plan.port, plan.width, plan.blocks, plan.reach, plan.own
    G, M, S = plan.groups, plan.group, plan.pieces
    dma = pltpu.SemaphoreType.DMA
    return pl.pallas_call(
        functools.partial(response_kernel, plan),
        out_shape=(
            jax.ShapeDtypeStruct((2, plan.line, G, M, plan.cycles), BF16),
            jax.ShapeDtypeStruct((2, plan.line * own, plan.ports), BF16),
        ),
        in_specs=[pl.BlockSpec(memory_space=pl.ANY)] * 6,
        out_specs=(pl.BlockSpec(memory_space=pltpu.VMEM), pl.BlockSpec(memory_space=pl.ANY)),
        scratch_shapes=[
            pltpu.VMEM(counters.shape, BF16),
            pltpu.VMEM(signatures.shape, BF16),
            pltpu.VMEM(eigen.shape, BF16),
            pltpu.VMEM(taps.shape, BF16),
            pltpu.VMEM(forward.shape, BF16),
            pltpu.VMEM(inverse.shape, BF16),
            pltpu.VMEM((N * own, plan.tallies), F32),
            pltpu.VMEM((N, plan.rows, plan.tallies), F32),
            pltpu.VMEM((plan.ways, plan.rows, plan.tallies), F32),
            pltpu.VMEM((R + 1, G, M, plan.cycles), BF16),
            pltpu.VMEM(((R + 1) * C, M, 2 * W), F32),
            pltpu.VMEM((plan.lags, own, 2 * W), F32),
            pltpu.VMEM((C, M, 2 * W), F32),
            pltpu.VMEM((2, plan.line * own, plan.ports), BF16),
            dma((6,)), dma((N,)), dma((N,)), dma((plan.ways,)), dma((plan.ways,)),
            dma((R + 1, G)), dma((R + 1, G)), dma((N, G * S, 4)), dma((N, G * S)), dma,
        ],
        compiler_params=pltpu.CompilerParams(
            collective_id=0, has_side_effects=True, vmem_limit_bytes=LARGE_GRANT
        ),
        name="response",
    )(counters, signatures, eigen, taps, forward, inverse)


def sag_kernel(plan, response, turned, sag, held, vectors, rounded, load_sem, store_sem):
    W, C, modes = plan.width, plan.blocks, plan.port * plan.own
    vectors_load = pltpu.make_async_copy(turned, vectors, load_sem.at[C])
    loads = [
        pltpu.make_async_copy(
            response.at[:, :, :, :, pl.ds(a * W, W)], held.at[a], load_sem.at[a]
        )
        for a in range(C)
    ]
    loads[0].start()
    vectors_load.start()
    for load in loads[1:]:
        load.start()
    stores = []
    for a in range(C):
        loads[a].wait()
        block = held[a].reshape(modes, W).T
        if a == 0:
            vectors_load.wait()
        rows = pl.ds(a * W, W)
        rounded[rows] = dot(block, vectors[...].reshape(modes, plan.ports)).astype(BF16)
        stores.append(pltpu.make_async_copy(rounded.at[rows], sag.at[rows], store_sem.at[a]))
        stores[a].start()
    for store in stores:
        store.wait()


def sag_call(plan, response, turned):
    line, G, M = plan.line, plan.groups, plan.group
    return pl.pallas_call(
        functools.partial(sag_kernel, plan),
        out_shape=jax.ShapeDtypeStruct((plan.cycles, plan.ports), BF16),
        in_specs=[pl.BlockSpec(memory_space=pl.ANY)] * 2,
        out_specs=pl.BlockSpec(memory_space=pl.ANY),
        scratch_shapes=[
            pltpu.VMEM((plan.blocks, 2, line, G, M, plan.width), BF16),
            pltpu.VMEM(turned.shape, BF16),
            pltpu.VMEM((plan.cycles, plan.ports), BF16),
            pltpu.SemaphoreType.DMA((plan.blocks + 1,)),
            pltpu.SemaphoreType.DMA((plan.blocks,)),
        ],
        compiler_params=pltpu.CompilerParams(vmem_limit_bytes=LARGE_GRANT),
        name="sag",
    )(response, turned)


def solution(mesh):
    def per_device(counters, signatures, eigen, taps):
        plan = Plan(
            mesh.shape["tm"], mesh.shape["port"], counters.shape[0], eigen.shape[0],
            counters.shape[1], taps.shape[0], taps.shape[1],
        )
        forward, inverse = odd_dft(plan.width)
        response, turned = response_call(
            plan, counters, signatures, eigen, taps, jnp.asarray(forward), jnp.asarray(inverse)
        )
        return sag_call(plan, response, turned)

    in_specs = (P("tm", None), P(None, "port"), P("port", None), P("port", None))
    return jax.shard_map(
        per_device, mesh=mesh, in_specs=in_specs, out_specs=P("tm", "port"), check_vma=False
    )
```

```python
import functools

import jax
import jax.numpy as jnp
import ml_dtypes
import numpy as np
from jax import lax
from jax.experimental import pallas as pl
from jax.experimental.pallas import tpu as pltpu
from jax.sharding import PartitionSpec as P

MESH = pl.DeviceIdType.MESH
LARGE_GRANT = 60 * 1024 * 1024
F32 = jnp.float32
BF16 = jnp.bfloat16
NT = (((1,), (1,)), ((), ()))
TN = (((0,), (0,)), ((), ()))


def split_parts(x):
    high = x.astype(ml_dtypes.bfloat16)
    low = (x - high.astype(np.float64)).astype(ml_dtypes.bfloat16)
    return high, low


def odd_dft(width):
    theta = np.pi * (2 * np.arange(width) + 1) / (2 * width)
    phase = np.outer(np.arange(width), theta)
    forward = np.concatenate([np.cos(phase), -np.sin(phase)], axis=1)
    phase = np.outer(theta, width + np.arange(width))
    inverse = np.concatenate([np.cos(phase), -np.sin(phase)], axis=0) / width
    return np.concatenate(split_parts(forward), axis=0), np.concatenate(split_parts(inverse), axis=0)


def halves(x):
    high = x.astype(BF16)
    return high, (x - high.astype(F32)).astype(BF16)


def dot(a, b):
    return jnp.dot(a, b, preferred_element_type=F32)


class Plan:
    def __init__(self, tm, port, cycles, ports, tallies, own, span):
        self.tm, self.port, self.cycles, self.ports, self.tallies = tm, port, cycles, ports, tallies
        self.own, self.span = own, span
        self.width = min(256, cycles)
        self.blocks = cycles // self.width
        self.lags = span // self.width
        self.reach = min((span - 2) // cycles + 1, tm - 1)
        self.ways = min(tm, own // 8)
        self.rows = own // self.ways
        self.line = port // 2
        self.group = min(16, own)
        self.groups = own // self.group
        self.pieces = 2


def response_kernel(
    plan, counters, signatures, eigen, taps, forward, inverse, out, turned_out,
    cnt, sig, eig, tap, fwd, inv, partial, parts, merged, xs, spectra, taps_spectra, product, turned,
    load_sem, part_send, part_recv, merged_send, merged_recv, modal_send, modal_recv, out_send, out_recv, turned_sem,
):
    T, N, W, C, R, own = plan.tm, plan.port, plan.width, plan.blocks, plan.reach, plan.own
    G, M = plan.groups, plan.group
    t, p = lax.axis_index("tm"), lax.axis_index("port")
    loads = [
        pltpu.make_async_copy(src, dst, load_sem.at[i])
        for i, (src, dst) in enumerate(
            [(signatures, sig), (eigen, eig), (forward, fwd), (taps, tap), (counters, cnt), (inverse, inv)]
        )
    ]
    for load in loads:
        load.start()

    barrier = pltpu.get_barrier_semaphore()
    for k in range(1, N):
        pl.semaphore_signal(
            barrier, inc=1, device_id={"tm": t, "port": lax.rem(p + k, N)}, device_id_type=MESH
        )
    greeted = N - 1
    for k in range(1, R + 1):
        @pl.when(t + k < T)
        def _():
            pl.semaphore_signal(barrier, inc=1, device_id={"tm": t + k, "port": p}, device_id_type=MESH)

        @pl.when(t - k >= 0)
        def _():
            pl.semaphore_signal(barrier, inc=1, device_id={"tm": t - k, "port": p}, device_id_type=MESH)

        greeted = greeted + jnp.where(t + k < T, 1, 0) + jnp.where(t - k >= 0, 1, 0)

    loads[0].wait()
    loads[1].wait()
    partial[...] = dot(sig[...], eig[...]).T
    pl.semaphore_wait(barrier, greeted)

    share = lax.rem(t, plan.ways)

    def part_copy(k):
        to = lax.rem(p + k, N)
        return pltpu.make_async_remote_copy(
            src_ref=partial.at[pl.ds(pl.multiple_of(to * own + share * plan.rows, 8), plan.rows)],
            dst_ref=parts.at[k],
            send_sem=part_send.at[k],
            recv_sem=part_recv.at[k],
            device_id={"tm": t, "port": to},
            device_id_type=MESH,
        )

    for k in range(1, N):
        part_copy(k).start()

    loads[2].wait()
    loads[3].wait()

    def transform(x):
        return dot(x, fwd[:W]) + dot(x, fwd[W:])

    quad = 4

    def taps_step(i, carry):
        rows = [tap[:, pl.ds(pl.multiple_of((i * quad + j) * W, W), W)] for j in range(quad)]
        result = transform(jnp.concatenate(rows, axis=0))
        taps_spectra[pl.ds(i * quad, quad)] = result.reshape(quad, own, 2 * W)
        return carry

    steps = plan.lags // quad
    lax.fori_loop(0, steps // 2, taps_step, 0)
    for d in range(1, R + 1):
        @pl.when(t < d)
        def _():
            xs[d] = jnp.zeros_like(xs[d])

    octet = partial[pl.ds(pl.multiple_of(p * own + share * plan.rows, 8), plan.rows)]
    for k in range(1, N):
        part_copy(k).wait_recv()
        octet = octet + parts[k]
    merged[share] = octet

    def merged_copy(k):
        mate = t - share + lax.rem(share + k, plan.ways)
        return pltpu.make_async_remote_copy(
            src_ref=merged.at[share],
            dst_ref=merged.at[share],
            send_sem=merged_send.at[k],
            recv_sem=merged_recv.at[k],
            device_id={"tm": mate, "port": p},
            device_id_type=MESH,
        )

    for k in range(1, plan.ways):
        merged_copy(k).start()
    lax.fori_loop(steps // 2, steps, taps_step, 0)
    loads[4].wait()
    for k in range(1, plan.ways):
        came = lax.rem(share + plan.ways - k, plan.ways)
        pltpu.make_async_remote_copy(
            src_ref=merged.at[came], dst_ref=merged.at[came], send_sem=merged_send.at[k],
            recv_sem=merged_recv.at[k], device_id={"tm": t - share + came, "port": p}, device_id_type=MESH,
        ).wait_recv()

    high, low = halves(merged[...].reshape(own, plan.tallies))
    both = lax.dot_general(jnp.concatenate([high, low], axis=0), cnt[...], NT, preferred_element_type=F32)
    modal = (both[:own] + both[own:]).astype(BF16)
    xs[0] = modal.reshape(G, M, plan.cycles)

    def modal_copy(d, h):
        return pltpu.make_async_remote_copy(
            src_ref=xs.at[0, h],
            dst_ref=xs.at[d, h],
            send_sem=modal_send.at[d, h],
            recv_sem=modal_recv.at[d, h],
            device_id={"tm": t + d, "port": p},
            device_id_type=MESH,
        )

    for h in range(G):
        for d in range(1, R + 1):
            @pl.when(t + d < T)
            def _():
                modal_copy(d, h).start()

    tile = min(256, plan.ports)
    for i in range(plan.ports // tile):
        block = eig[i * tile : (i + 1) * tile].T
        for piece in range(N):
            z, b = divmod(piece, 2)
            turned[b, z * own : (z + 1) * own, i * tile : (i + 1) * tile] = block[piece * own : (piece + 1) * own]
    turned_copy = pltpu.make_async_copy(turned, turned_out, turned_sem)
    turned_copy.start()

    sign = 1.0 - 2.0 * (lax.broadcasted_iota(jnp.int32, (8, 128), 1) % 2).astype(F32)

    def product_step(h, g):
        rows = pl.ds(pl.multiple_of(g * 8, 8), 8)
        taps_rows = pl.ds(pl.multiple_of(h * M + g * 8, 8), 8)
        for q in range(W // 128):
            re, im = slice(q * 128, q * 128 + 128), slice(W + q * 128, W + q * 128 + 128)
            acc_re, acc_im = [None] * C, [None] * C
            before = None
            for j in range(-R * C, C):
                now = (spectra[R * C + j, rows, re], spectra[R * C + j, rows, im])
                z_re, z_im = sign * now[1], -(sign * now[0])
                if before is not None:
                    z_re, z_im = z_re + before[0], z_im + before[1]
                before = now
                for a in range(C):
                    lag = a - j
                    if 0 <= lag < plan.lags:
                        h_re, h_im = taps_spectra[lag, taps_rows, re], taps_spectra[lag, taps_rows, im]
                        add_re, add_im = h_re * z_re - h_im * z_im, h_re * z_im + h_im * z_re
                        acc_re[a] = add_re if acc_re[a] is None else acc_re[a] + add_re
                        acc_im[a] = add_im if acc_im[a] is None else acc_im[a] + add_im
            for a in range(C):
                product[a, rows, re] = acc_re[a]
                product[a, rows, im] = acc_im[a]

    place, side = p // 2, lax.rem(p, 2)
    S = plan.pieces
    wide = plan.cycles // S
    up, down, partner, across = 0, 1, 2, 3
    mate = p + 1 - 2 * side
    pair = place + 1 - 2 * lax.rem(place, 2)
    paired = 2 * pair + side

    def out_copy(piece, i, way, to):
        h = i // S
        c = lax.rem(i, S)
        part = out.at[lax.rem(piece, 2), piece // 2, h, :, pl.ds(pl.multiple_of(c * wide, wide), wide)]
        return pltpu.make_async_remote_copy(
            src_ref=part,
            dst_ref=part,
            send_sem=out_send.at[piece, i, way],
            recv_sem=out_recv.at[piece, i],
            device_id={"tm": t, "port": to},
            device_id_type=MESH,
        )

    loads[5].wait()

    def group_step(h, carry):
        for d in range(1, R + 1):
            @pl.when(t >= d)
            def _():
                modal_copy(d, h).wait_recv()

        rows = [
            xs[d, h, :, i * W : (i + 1) * W] for d in range(R, -1, -1) for i in range(C)
        ]
        spectra[...] = transform(jnp.concatenate(rows, axis=0)).reshape((R + 1) * C, M, 2 * W)

        def step(g, inner):
            product_step(h, g)
            return inner

        lax.fori_loop(0, M // 8, step, 0)
        high, low = halves(product[...].reshape(C * M, 2 * W))
        result = dot(high, inv[: 2 * W]) + dot(low, inv[: 2 * W]) + dot(high, inv[2 * W :])
        result = result.astype(BF16)
        for a in range(C):
            out[side, place, h, :, a * W : (a + 1) * W] = result[a * M : (a + 1) * M]

        for c in range(S):
            i = h * S + c

            @pl.when(place + 1 < plan.line)
            def _():
                out_copy(p, i, up, p + 2).start()

            @pl.when(place >= 1)
            def _():
                out_copy(p, i, down, p - 2).start()

            out_copy(p, i, partner, mate).start()

        return carry

    lax.fori_loop(0, G, group_step, 0)

    for k in range(1, plan.line):
        def forward_step(i, carry):
            @pl.when(place >= k)
            def _():
                piece = p - 2 * k
                out_copy(piece, i, up, mate).wait_recv()

                @pl.when(place + 1 < plan.line)
                def _():
                    out_copy(piece, i, up, p + 2).start()

                @pl.when((piece != paired) | (lax.rem(i, 2) == 0))
                def _():
                    out_copy(piece, i, partner, mate).start()

            @pl.when(place + k < plan.line)
            def _():
                piece = p + 2 * k
                out_copy(piece, i, down, mate).wait_recv()

                @pl.when(place >= 1)
                def _():
                    out_copy(piece, i, down, p - 2).start()

                @pl.when((piece != paired) | (lax.rem(i, 2) == 0))
                def _():
                    out_copy(piece, i, partner, mate).start()

            if k == 1:
                @pl.when(lax.rem(i, 2) == 1)
                def _():
                    out_copy(mate, i, across, mate).wait_recv()
                    out_copy(mate, i, across, paired).start()

            return carry

        lax.fori_loop(0, G * S, forward_step, 0)

    def arrived(n, carry):
        i = lax.rem(n, G * S)
        z = n // (G * S)

        @pl.when((z != place) | (lax.rem(i, 2) == 0))
        def _():
            out_copy(2 * z + 1 - side, i, partner, mate).wait_recv()

        return carry

    lax.fori_loop(0, plan.line * G * S, arrived, 0)

    def finish(n, carry):
        i = lax.rem(n, G * S)
        z = n // (G * S)
        piece = 2 * z + side

        @pl.when((z != pair) | (lax.rem(i, 2) == 0))
        def _():
            out_copy(piece, i, partner, mate).wait_send()

        @pl.when((z == place) & (lax.rem(i, 2) == 1))
        def _():
            out_copy(mate, i, across, mate).wait_send()

        @pl.when((z <= place) & (place + 1 < plan.line))
        def _():
            out_copy(piece, i, up, mate).wait_send()

        @pl.when((z >= place) & (place >= 1))
        def _():
            out_copy(piece, i, down, mate).wait_send()

        return carry

    lax.fori_loop(0, plan.line * G * S, finish, 0)
    turned_copy.wait()
    for k in range(1, N):
        part_copy(k).wait_send()
    for k in range(1, plan.ways):
        merged_copy(k).wait_send()
    for d in range(1, R + 1):
        @pl.when(t + d < T)
        def _():
            for h in range(G):
                modal_copy(d, h).wait_send()


def response_call(plan, counters, signatures, eigen, taps, forward, inverse):
    T, N, W, C, R, own = plan.tm, plan.port, plan.width, plan.blocks, plan.reach, plan.own
    G, M, S = plan.groups, plan.group, plan.pieces
    dma = pltpu.SemaphoreType.DMA
    return pl.pallas_call(
        functools.partial(response_kernel, plan),
        out_shape=(
            jax.ShapeDtypeStruct((2, plan.line, G, M, plan.cycles), BF16),
            jax.ShapeDtypeStruct((2, plan.line * own, plan.ports), BF16),
        ),
        in_specs=[pl.BlockSpec(memory_space=pl.ANY)] * 6,
        out_specs=(pl.BlockSpec(memory_space=pltpu.VMEM), pl.BlockSpec(memory_space=pl.ANY)),
        scratch_shapes=[
            pltpu.VMEM(counters.shape, BF16),
            pltpu.VMEM(signatures.shape, BF16),
            pltpu.VMEM(eigen.shape, BF16),
            pltpu.VMEM(taps.shape, BF16),
            pltpu.VMEM(forward.shape, BF16),
            pltpu.VMEM(inverse.shape, BF16),
            pltpu.VMEM((N * own, plan.tallies), F32),
            pltpu.VMEM((N, plan.rows, plan.tallies), F32),
            pltpu.VMEM((plan.ways, plan.rows, plan.tallies), F32),
            pltpu.VMEM((R + 1, G, M, plan.cycles), BF16),
            pltpu.VMEM(((R + 1) * C, M, 2 * W), F32),
            pltpu.VMEM((plan.lags, own, 2 * W), F32),
            pltpu.VMEM((C, M, 2 * W), F32),
            pltpu.VMEM((2, plan.line * own, plan.ports), BF16),
            dma((6,)), dma((N,)), dma((N,)), dma((plan.ways,)), dma((plan.ways,)),
            dma((R + 1, G)), dma((R + 1, G)), dma((N, G * S, 4)), dma((N, G * S)), dma,
        ],
        compiler_params=pltpu.CompilerParams(
            collective_id=0, has_side_effects=True, vmem_limit_bytes=LARGE_GRANT
        ),
        name="response",
    )(counters, signatures, eigen, taps, forward, inverse)


def sag_kernel(plan, response, turned, sag, held, vectors, rounded, load_sem, store_sem):
    W, C, modes = plan.width, plan.blocks, plan.port * plan.own
    vectors_load = pltpu.make_async_copy(turned, vectors, load_sem.at[C])
    loads = [
        pltpu.make_async_copy(
            response.at[:, :, :, :, pl.ds(a * W, W)], held.at[a], load_sem.at[a]
        )
        for a in range(C)
    ]
    loads[0].start()
    vectors_load.start()
    for load in loads[1:]:
        load.start()
    stores = []
    for a in range(C):
        loads[a].wait()
        block = held[a].reshape(modes, W).T
        if a == 0:
            vectors_load.wait()
        rows = pl.ds(a * W, W)
        rounded[rows] = dot(block, vectors[...].reshape(modes, plan.ports)).astype(BF16)
        stores.append(pltpu.make_async_copy(rounded.at[rows], sag.at[rows], store_sem.at[a]))
        stores[a].start()
    for store in stores:
        store.wait()


def sag_call(plan, response, turned):
    line, G, M = plan.line, plan.groups, plan.group
    return pl.pallas_call(
        functools.partial(sag_kernel, plan),
        out_shape=jax.ShapeDtypeStruct((plan.cycles, plan.ports), BF16),
        in_specs=[pl.BlockSpec(memory_space=pl.ANY)] * 2,
        out_specs=pl.BlockSpec(memory_space=pl.ANY),
        scratch_shapes=[
            pltpu.VMEM((plan.blocks, 2, line, G, M, plan.width), BF16),
            pltpu.VMEM(turned.shape, BF16),
            pltpu.VMEM((plan.cycles, plan.ports), BF16),
            pltpu.SemaphoreType.DMA((plan.blocks + 1,)),
            pltpu.SemaphoreType.DMA((plan.blocks,)),
        ],
        compiler_params=pltpu.CompilerParams(vmem_limit_bytes=LARGE_GRANT),
        name="sag",
    )(response, turned)


def solution(mesh):
    def per_device(counters, signatures, eigen, taps):
        plan = Plan(
            mesh.shape["tm"], mesh.shape["port"], counters.shape[0], eigen.shape[0],
            counters.shape[1], taps.shape[0], taps.shape[1],
        )
        forward, inverse = odd_dft(plan.width)
        response, turned = response_call(
            plan, counters, signatures, eigen, taps, jnp.asarray(forward), jnp.asarray(inverse)
        )
        return sag_call(plan, response, turned)

    in_specs = (P("tm", None), P(None, "port"), P("port", None), P("port", None))
    return jax.shard_map(
        per_device, mesh=mesh, in_specs=in_specs, out_specs=P("tm", "port"), check_vma=False
    )
```
